512 devices in a mesh: elem: 128 (over x_hi, z, y), lev: 4 (over x_lo, core).
Axes of the slice: x: 4 (x_hi: 2, x_lo: 2; x = x_hi * 2 + x_lo), y: 8, z: 8, core: 2. Of those that a mesh axis runs over, the one named last changes fastest.
Arguments:
- thermal_anomaly: float32 [72, 16, 65536], P('lev', None, 'elem'), may hold values from -6 to 6
- zonal_velocity: bfloat16 [72, 16, 65536], P('lev', None, 'elem'), may hold values from -6 to 6
- meridional_velocity: bfloat16 [72, 16, 65536], P('lev', None, 'elem'), may hold values from -6 to 6
- patch_mesh_position: int32 [128, 512], P('elem'), may hold values from 0 to 511, each once within a row
- sunlit_mask: int32 [65536], P('elem'), may hold values from 0 to 1, as said below
- entry_matrix: bfloat16 [512, 72], replicated, may hold values from -0.75 to 0.75
- entry_offset: float32 [512], replicated, may hold values from -6 to 6
- inner_matrices: bfloat16 [2, 512, 512], replicated, may hold values from -0.25 to 0.25
- inner_offsets: float32 [2, 512], replicated, may hold values from -6 to 6
- readout_matrix: bfloat16 [72, 512], replicated, may hold values from -0.25 to 0.25
Outputs:
- temperature_out: float32 [72, 16, 65536], P('lev', None, 'elem')
The draws below stay inside these ranges and needn't reach their ends.
Inputs may be any that keep to these rules, and one draw needn't show every extreme that they name: `sunlit_mask`: the flags of element e and of element e + 32768 sum to one. `patch_mesh_position`: each row is an ordering of the 512 grid slots of one device.
All inputs are finite; a program needn't handle non-finite values.
Results may differ from the reference program's by a relative error of at most 0.0028.
Values may be sent and summed in bfloat16 or wider, within the bound.
A program may use at most 64 MiB of HBM per device.

```python
import math
import jax
import jax.numpy as jnp
from jax import lax

LAYER_NUMBER = 72
UNITS = 512
MID = 2
EDGE_QUADRATURE = 4
ELEMENTS_FIRST = 8
ELEMENTS_SECOND = 64
ELEMS_DEV = 512
PATCH_SUM = 65536
N_ELEM = 128


def draw_sunlit_mask(key, part):
    key = jax.random.fold_in(key, 7)
    accelerator_list = PATCH_SUM // ELEMS_DEV
    half = accelerator_list // 2
    thresholds = 10 + 80 * jnp.arange(half, dtype=jnp.int32) // max(half - 1, 1)
    samples = jax.random.randint(key, (half, ELEMS_DEV), 0, 100)
    daylit_half = (samples < thresholds[:, None]).astype(jnp.int32).reshape(-1)
    return jnp.concatenate([daylit_half, 1 - daylit_half])


def block_scale(rng, extent, split, smallest, largest):
    level = 1.0
    for axis_at, shards_of in split:
        steps = jax.random.uniform(jax.random.fold_in(jax.random.fold_in(rng, 6), axis_at), (shards_of,), jnp.float32, smallest / len(split), largest / len(split))
        level = level * jnp.repeat(jnp.exp(steps), extent[axis_at] // shards_of).reshape((-1,) + (1,) * (len(extent) - 1 - axis_at))
    return level


def centred(key, shape, spread, reach, shards=(), kind=jnp.bfloat16):
    loudness = block_scale(key, shape, shards, -0.22, 0.18) if shards else 1.0
    values = jax.random.normal(key, shape, jnp.float32) * spread * loudness
    return jnp.minimum(jnp.maximum(values, -reach), reach).astype(kind)


def setup_inputs(seed: int = 0) -> dict:
    splits = jax.random.split(jax.random.key(seed), 11)
    return {
        "thermal_anomaly": centred(splits[0], (LAYER_NUMBER, EDGE_QUADRATURE * EDGE_QUADRATURE, PATCH_SUM), 1.0, 6.0, ((0, 4), (2, 128)), jnp.float32),
        "zonal_velocity": centred(splits[1], (LAYER_NUMBER, EDGE_QUADRATURE * EDGE_QUADRATURE, PATCH_SUM), 1.0, 6.0, ((0, 4), (2, 128))),
        "meridional_velocity": centred(splits[2], (LAYER_NUMBER, EDGE_QUADRATURE * EDGE_QUADRATURE, PATCH_SUM), 1.0, 6.0, ((0, 4), (2, 128))),
        "patch_mesh_position": jax.vmap(lambda own: jax.random.permutation(own, ELEMS_DEV))(jax.random.split(splits[3], N_ELEM)).reshape((N_ELEM, ELEMS_DEV)).astype(jnp.int32),
        "sunlit_mask": draw_sunlit_mask(jax.random.fold_in(splits[10], 71), 0),
        "entry_matrix": centred(splits[5], (UNITS, LAYER_NUMBER), LAYER_NUMBER ** -0.5, 0.75),
        "entry_offset": centred(splits[6], (UNITS,), 1.0, 6.0, (), jnp.float32),
        "inner_matrices": centred(splits[7], (MID, UNITS, UNITS), UNITS ** -0.5, 0.25),
        "inner_offsets": centred(splits[8], (MID, UNITS), 1.0, 6.0, (), jnp.float32),
        "readout_matrix": centred(splits[9], (LAYER_NUMBER, UNITS), UNITS ** -0.5, 0.25),
    }


def derivative_table():
    gll_nodes = [-1.0, -1.0 / math.sqrt(5.0), 1.0 / math.sqrt(5.0), 1.0]
    table_rows = []
    for i in range(4):
        one_row = []
        for j in range(4):
            if i == j:
                entry_value = sum((1.0 / (gll_nodes[i] - gll_nodes[m]) for m in range(4) if m != i))
            else:
                upper_part = 1.0
                lower_part = 1.0
                for m in range(4):
                    if m != i and m != j:
                        upper_part = upper_part * (gll_nodes[i] - gll_nodes[m])
                    if m != j:
                        lower_part = lower_part * (gll_nodes[j] - gll_nodes[m])
                entry_value = upper_part / lower_part
            one_row.append(entry_value)
        table_rows.append(one_row)
    return jnp.array(table_rows, jnp.float32)

def along_first(table, field):
    return jnp.einsum('ik,lkjxy->lijxy', table, field, precision=lax.Precision.HIGHEST)

def along_second(table, field):
    return jnp.einsum('jk,likxy->lijxy', table, field, precision=lax.Precision.HIGHEST)

def compute_rate_change(temp_grid, wind_u, wind_v):
    table = derivative_table()
    grad_x = along_first(table, temp_grid)
    grad_y = along_second(table, temp_grid)
    curve = along_first(table, grad_x) + along_second(table, grad_y)
    return -(wind_u * grad_x + wind_v * grad_y) + 0.1 * curve

def mean_along_abscissa(field):
    upper = field[:, 3]
    lower = jnp.roll(field[:, 0], -1, axis=2)
    middle = (upper + lower) * 0.5
    return field.at[:, 3].set(middle).at[:, 0].set(jnp.roll(middle, 1, axis=2))

def mean_along_ordinate(field):
    upper = field[:, :, 3]
    lower = jnp.roll(field[:, :, 0], -1, axis=3)
    middle = (upper + lower) * 0.5
    return field.at[:, :, 3].set(middle).at[:, :, 0].set(jnp.roll(middle, 1, axis=3))

def permute_patches(field, patch_permutation_map, accelerator_list):
    neural_layer_number = field.shape[0]
    blocks = field.reshape(neural_layer_number, EDGE_QUADRATURE * EDGE_QUADRATURE, accelerator_list, ELEMS_DEV)
    picked = jnp.take_along_axis(blocks, jnp.broadcast_to(patch_permutation_map[None, None], blocks.shape), axis=3)
    return picked.reshape(neural_layer_number, EDGE_QUADRATURE, EDGE_QUADRATURE, accelerator_list * ELEMENTS_FIRST, ELEMENTS_SECOND)

def unpermute_patches(grid, patch_mesh_position, accelerator_list):
    neural_layer_number = grid.shape[0]
    blocks = grid.reshape(neural_layer_number, EDGE_QUADRATURE * EDGE_QUADRATURE, accelerator_list, ELEMS_DEV)
    picked = jnp.take_along_axis(blocks, jnp.broadcast_to(patch_mesh_position[None, None], blocks.shape), axis=3)
    return picked.reshape(neural_layer_number, EDGE_QUADRATURE * EDGE_QUADRATURE, accelerator_list * ELEMS_DEV)

def radiate(column, entry_matrix, entry_offset, inner_matrices, inner_offsets, readout_matrix):
    hidden = jax.nn.silu(jnp.dot(entry_matrix, column, preferred_element_type=jnp.float32) + entry_offset[:, None]).astype(jnp.bfloat16)
    for m in range(MID):
        hidden = jax.nn.silu(jnp.dot(inner_matrices[m], hidden, preferred_element_type=jnp.float32) + inner_offsets[m][:, None]).astype(jnp.bfloat16)
    return jnp.dot(readout_matrix, hidden, preferred_element_type=jnp.float32)

def reference(thermal_anomaly, zonal_velocity, meridional_velocity, patch_mesh_position, sunlit_mask, entry_matrix, entry_offset, inner_matrices, inner_offsets, readout_matrix):
    accelerator_list = PATCH_SUM // ELEMS_DEV
    slots = jnp.broadcast_to(jnp.arange(ELEMS_DEV, dtype=jnp.int32)[None, :], (accelerator_list, ELEMS_DEV))
    patch_permutation_map = jnp.zeros((accelerator_list, ELEMS_DEV), jnp.int32).at[jnp.arange(accelerator_list, dtype=jnp.int32)[:, None], patch_mesh_position].set(slots)

    def lone_stratum(fields):
        stratum_warmth, along_u, along_v = fields
        mesh_thermal_anomaly = permute_patches(stratum_warmth[None], patch_permutation_map, accelerator_list)
        mesh_zonal_velocity = permute_patches(along_u[None].astype(jnp.float32), patch_permutation_map, accelerator_list)
        mesh_meridional_velocity = permute_patches(along_v[None].astype(jnp.float32), patch_permutation_map, accelerator_list)
        rate_change = mean_along_ordinate(mean_along_abscissa(compute_rate_change(mesh_thermal_anomaly, mesh_zonal_velocity, mesh_meridional_velocity)))
        return unpermute_patches(mesh_thermal_anomaly + 0.05 * rate_change, patch_mesh_position, accelerator_list)[0]
    advance_timestep = lax.map(lone_stratum, (thermal_anomaly, zonal_velocity, meridional_velocity))
    column = advance_timestep.astype(jnp.bfloat16).reshape(LAYER_NUMBER, EDGE_QUADRATURE * EDGE_QUADRATURE, accelerator_list, ELEMS_DEV).transpose(2, 0, 1, 3)
    flags = sunlit_mask.reshape(accelerator_list, ELEMS_DEV).astype(jnp.float32)

    def one_block(pair):
        block_column, block_flags = pair
        heat = radiate(block_column.reshape(LAYER_NUMBER, EDGE_QUADRATURE * EDGE_QUADRATURE * ELEMS_DEV), entry_matrix, entry_offset, inner_matrices, inner_offsets, readout_matrix)
        heat = heat.reshape(LAYER_NUMBER, EDGE_QUADRATURE * EDGE_QUADRATURE, ELEMS_DEV)
        return (heat * block_flags[None, None, :]).astype(jnp.bfloat16)
    heating = lax.map(one_block, (column, flags)).transpose(1, 2, 0, 3).reshape(LAYER_NUMBER, EDGE_QUADRATURE * EDGE_QUADRATURE, PATCH_SUM)
    return advance_timestep + heating.astype(jnp.float32)
```

```python
import functools
import math

import jax
import jax.numpy as jnp
import numpy as np
from jax import lax
from jax.experimental import pallas as pl
from jax.experimental.pallas import tpu as pltpu
from jax.sharding import PartitionSpec as P

MESH = pl.DeviceIdType.MESH
F32 = jnp.float32
BF16 = jnp.bfloat16
LEV = 4
NL = 18
NODES = 16
ROWS = NL * NODES
NE = 512
HALF = ROWS // 2
LEVELS = NL * LEV
UNITS = 512
NT = (((1,), (1,)), ((), ()))


def derivative_table():
    nodes = [-1.0, -1.0 / math.sqrt(5.0), 1.0 / math.sqrt(5.0), 1.0]
    table = np.zeros((4, 4))
    for i in range(4):
        for j in range(4):
            if i == j:
                table[i, j] = sum(1.0 / (nodes[i] - nodes[m]) for m in range(4) if m != i)
            else:
                upper = lower = 1.0
                for m in range(4):
                    if m != i and m != j:
                        upper *= nodes[i] - nodes[m]
                    if m != j:
                        lower *= nodes[j] - nodes[m]
                table[i, j] = upper / lower
    return table


def derivative_blocks():
    table = derivative_table()
    eye4, eye9 = np.eye(4), np.eye(HALF // NODES)
    first = np.kron(table, eye4)
    second = np.kron(eye4, table)
    blocks = [0.05 * first, 0.05 * second, 0.005 * (first @ first + second @ second)]
    return np.concatenate([np.kron(eye9, b) for b in blocks]).astype(np.float32)


def kernel(
    t_hbm, u_hbm, v_hbm, pos_hbm, flag_hbm, d_hbm, w0_hbm, b0_hbm, wi_hbm, bi_hbm, wr_hbm,
    out_hbm,
    t_v, u_v, v_v, pos_v, flag_v, d_v, w0_v, b0_v, wi_v, bi_v, wr_v,
    q_s, tg_s, ag_s, dd_s, fl_s, w0_s, wi_s, bias_s,
    halo_s, halo_out, halo_in, col_s, col_out, col_in, x_s, h_s, heat_out, heat_in, hin_s, sum_s, out_v,
    in_sem, out_sem, halo_send, halo_recv, col_send, col_recv, heat_send, heat_recv,
):
    me = lax.axis_index("lev")
    elem = lax.axis_index("elem")
    count = lax.axis_size("elem")
    nxt = lax.rem(elem + 1, count)
    prv = lax.rem(elem + count - 1, count)
    peers = [lax.rem(me + d, LEV) for d in (2, 1, 3)]

    loads = {}
    pairs = [
        ("pos", pos_hbm, pos_v), ("t", t_hbm, t_v), ("d", d_hbm, d_v), ("u", u_hbm, u_v),
        ("v", v_hbm, v_v), ("flag", flag_hbm, flag_v), ("w0", w0_hbm, w0_v), ("b0", b0_hbm, b0_v),
        ("bi", bi_hbm, bi_v), ("wi", wi_hbm, wi_v), ("wr", wr_hbm, wr_v),
    ]
    for n, (name, src, dst) in enumerate(pairs):
        loads[name] = pltpu.make_async_copy(src, dst, in_sem.at[n])
        loads[name].start()

    barrier = pltpu.get_barrier_semaphore()
    for p in peers:
        pl.semaphore_signal(barrier, inc=1, device_id=(elem, p), device_id_type=MESH)
    for e in (nxt, prv):
        pl.semaphore_signal(barrier, inc=1, device_id=(e, me), device_id_type=MESH)

    loads["pos"].wait()
    slot = lax.rem(pos_v[...] + 64, NE)
    for r in range(0, NE, 128):
        rows = lax.broadcasted_iota(jnp.int32, (128, NE), 0) + r
        q_s[pl.ds(r, 128), :] = jnp.where(rows == slot, 1.0, 0.0).astype(BF16)

    loads["t"].wait()
    loads["flag"].wait()
    flags = jnp.broadcast_to(flag_v[...].astype(F32), (16, NE)).astype(BF16)
    t_b = t_v[...].astype(BF16)
    both = lax.dot_general(
        jnp.concatenate([t_b, flags], axis=0), q_s[...], NT, preferred_element_type=F32
    )
    for c in range(4):
        ag_s[c] = both[:ROWS, 128 * c : 128 * c + 128]
    fl_s[...] = both[ROWS : ROWS + 8]

    loads["d"].wait()
    loads["u"].wait()
    loads["v"].wait()
    deriv = d_v[...].astype(BF16)
    parts = []
    for b in range(2):
        sl = slice(b * HALF, (b + 1) * HALF)
        g = jnp.dot(deriv, t_b[sl], preferred_element_type=F32)
        u = u_v[sl, :].astype(F32)
        v = v_v[sl, :].astype(F32)
        tend = g[2 * HALF :] - u * g[:HALF] - v * g[HALF : 2 * HALF]
        parts.append(tend.astype(BF16))
    tend = lax.dot_general(
        jnp.concatenate(parts, axis=0), q_s[...], NT, preferred_element_type=F32
    )
    for c in range(4):
        tg_s[c] = tend[:, 128 * c : 128 * c + 128]

    lane = lax.broadcasted_iota(jnp.int32, (NL, 128), 1)
    left = lane < 64
    inner = lane % 64

    def node(i, j, c):
        return tg_s[c, pl.ds(4 * i + j, NL, stride=NODES), :]

    halo_s[pl.ds(72, 8), :] = jnp.zeros((8, 128), F32)
    for j in range(4):
        halo_s[pl.ds(j, NL, stride=4), :] = jnp.where(left, node(3, j, 0), node(0, j, 0))
    halo_out[...] = halo_s[...].astype(BF16)
    pl.semaphore_wait(barrier, 5)
    halo_copies = []
    for n, e in enumerate((nxt, prv)):
        copy = pltpu.make_async_remote_copy(
            src_ref=halo_out, dst_ref=halo_in.at[n], send_sem=halo_send.at[n],
            recv_sem=halo_recv.at[n], device_id=(e, me), device_id_type=MESH,
        )
        copy.start()
        halo_copies.append(copy)

    def dss(c, halo):
        t = {(i, j): node(i, j, c) for i in range(4) for j in range(4)}
        for j in range(4):
            own0, own3 = t[0, j], t[3, j]
            near0, near3 = own0, own3
            if halo is not None:
                near3, near0 = halo[0][j], halo[1][j]
            after = pltpu.roll(jnp.where(left, node(0, j, (c + 1) % 4), near0), 64, 1)
            before = pltpu.roll(jnp.where(left, near3, node(3, j, (c + 3) % 4)), 64, 1)
            t[3, j] = (own3 + after) * 0.5
            t[0, j] = (own0 + before) * 0.5
        for i in range(4):
            own0, own3 = t[i, 0], t[i, 3]
            after = jnp.where(inner == 63, pltpu.roll(own0, 63, 1), pltpu.roll(own0, 127, 1))
            before = jnp.where(inner == 0, pltpu.roll(own3, 65, 1), pltpu.roll(own3, 1, 1))
            t[i, 3] = (own3 + after) * 0.5
            t[i, 0] = (own0 + before) * 0.5
        for i in range(4):
            for j in range(4):
                p = 4 * i + j
                dd_s[p, :NL, pl.ds(128 * c, 128)] = t[i, j]
                temp = ag_s[c, pl.ds(p, NL, stride=NODES), :]
                col_s[pl.ds(HALF * i + 72 * (c % 2) + j, NL, stride=4), :] = temp + t[i, j]

    col_copies = []

    def send_columns(s):
        col_out[s] = col_s[...].astype(BF16).reshape(LEV, HALF, 128)
        copies = []
        for n, p in enumerate(peers):
            copy = pltpu.make_async_remote_copy(
                src_ref=col_out.at[s, p], dst_ref=col_in.at[s, me], send_sem=col_send.at[s, n],
                recv_sem=col_recv.at[s, n], device_id=(elem, p), device_id_type=MESH,
            )
            copy.start()
            copies.append(copy)
        col_in[s, me] = col_out[s, me]
        col_copies.append(copies)

    dss(2, None)
    dss(3, None)
    send_columns(0)

    for copy in halo_copies:
        copy.wait_recv()
    from_before, from_after = [], []
    for n, store in enumerate((from_before, from_after)):
        halo_s[...] = halo_in[n].astype(F32)
        for j in range(4):
            store.append(halo_s[pl.ds(j, NL, stride=4), :])
    dss(0, (from_before, from_after))
    dss(1, None)
    send_columns(1)

    loads["w0"].wait()
    loads["b0"].wait()
    bias = b0_v[...] * 0.5
    coarse = bias.astype(BF16).astype(F32)
    row8 = lax.broadcasted_iota(jnp.int32, (8, UNITS), 0)
    tail = jnp.where(row8 == 0, coarse, jnp.where(row8 == 1, bias - coarse, 0.0))
    w0 = jnp.concatenate(
        [w0_v[...].astype(F32) * 0.5, tail, jnp.zeros((128 - LEVELS - 8, UNITS), F32)], axis=0
    )
    w0_s[...] = w0.T.astype(BF16)
    loads["bi"].wait()
    for m in range(2):
        bias_s[m] = jnp.broadcast_to(bi_v[pl.ds(m, 1), :] * 0.5, (128, UNITS)).T
    loads["wi"].wait()
    wi_s[...] = wi_v[...] * jnp.asarray(0.5, BF16)
    loads["wr"].wait()

    row8 = lax.broadcasted_iota(jnp.int32, (8, 256), 0)
    ones = jnp.where(row8 < 2, 1.0, 0.0)

    def gate(h):
        return (h + h * jnp.tanh(h)).astype(BF16)

    heat_copies = []
    for s in range(2):
        for copy in col_copies[s]:
            copy.wait_recv()
        for src in range(LEV):
            block = col_in[s, src].astype(F32)
            for h in range(2):
                x_s[pl.ds(288 * h + 72 * src, 72), :] = block[72 * h : 72 * h + 72]

        def step(j, carry):
            x = jnp.concatenate([x_s[pl.ds(288 * h + j, LEVELS, stride=4), :] for h in range(2)], axis=1)
            x = jnp.concatenate([x, ones], axis=0).astype(BF16)
            hid = gate(jnp.dot(w0_s[:, : LEVELS + 8], x, preferred_element_type=F32))
            for m in range(2):
                pre = jnp.dot(wi_s[pl.ds(m * UNITS, UNITS), :], hid, preferred_element_type=F32)
                off = bias_s[m]
                hid = gate(pre + jnp.concatenate([off, off], axis=1))
            heat = jnp.dot(wr_v[...], hid, preferred_element_type=F32)
            for h in range(2):
                h_s[pl.ds(288 * h + j, LEVELS, stride=4), :] = heat[:, 128 * h : 128 * h + 128]
            return carry

        lax.fori_loop(0, 4, step, 0)
        for dst in range(LEV):
            block = jnp.concatenate([h_s[pl.ds(288 * h + 72 * dst, 72), :] for h in range(2)], axis=0)
            heat_out[s, dst] = block.astype(BF16)
        copies = []
        for n, p in enumerate(peers):
            copy = pltpu.make_async_remote_copy(
                src_ref=heat_out.at[s, p], dst_ref=heat_in.at[s, me], send_sem=heat_send.at[s, n],
                recv_sem=heat_recv.at[s, n], device_id=(elem, p), device_id_type=MESH,
            )
            copy.start()
            copies.append(copy)
        heat_in[s, me] = heat_out[s, me]
        heat_copies.append(copies)

    for s in range(2):
        for copy in heat_copies[s]:
            copy.wait_recv()
        for q in range(LEV):
            hin_s[...] = heat_in[s, q].astype(F32)
            for h in range(2):
                c = 2 * (1 - s) + h
                lanes = pl.ds(128 * c, 128)
                day = fl_s[pl.ds(0, 1), lanes]
                for j in range(4):
                    p = 4 * q + j
                    heat = hin_s[pl.ds(72 * h + j, NL, stride=4), :]
                    sum_s[h, pl.ds(p, NL, stride=NODES), :] = dd_s[p, :NL, lanes] + heat * day
        lanes = pl.ds(256 * (1 - s), 256)
        total = jnp.concatenate([sum_s[0], sum_s[1]], axis=1).astype(BF16)
        back = jnp.dot(total, q_s[lanes, :], preferred_element_type=F32)
        if s == 0:
            out_v[...] = t_v[...] + back
        else:
            out_v[...] = out_v[...] + back
    store = pltpu.make_async_copy(out_v, out_hbm, out_sem)
    store.start()

    for copy in halo_copies:
        copy.wait_send()
    for copies in col_copies + heat_copies:
        for copy in copies:
            copy.wait_send()
    store.wait()


def on_device(t, u, v, pos, sunlit, w0, b0, wi, bi, wr):
    shape = t.shape
    args = [
        t.reshape(ROWS, NE), u.reshape(ROWS, NE), v.reshape(ROWS, NE), pos, sunlit.reshape(1, NE),
        jnp.asarray(derivative_blocks()), w0.T, b0.reshape(1, UNITS), wi.reshape(2 * UNITS, UNITS),
        bi, wr,
    ]
    vmem = [pltpu.VMEM(a.shape, a.dtype) for a in args]
    dma = pltpu.SemaphoreType.DMA
    scratch = vmem + [
        pltpu.VMEM((NE, NE), BF16),
        pltpu.VMEM((4, ROWS, 128), F32),
        pltpu.VMEM((4, ROWS, 128), F32),
        pltpu.VMEM((NODES, 24, NE), F32),
        pltpu.VMEM((8, NE), F32),
        pltpu.VMEM((UNITS, 128), BF16),
        pltpu.VMEM((2 * UNITS, UNITS), BF16),
        pltpu.VMEM((2, UNITS, 128), F32),
        pltpu.VMEM((80, 128), F32),
        pltpu.VMEM((80, 128), BF16),
        pltpu.VMEM((2, 80, 128), BF16),
        pltpu.VMEM((LEV * HALF, 128), F32),
        pltpu.VMEM((2, LEV, HALF, 128), BF16),
        pltpu.VMEM((2, LEV, HALF, 128), BF16),
        pltpu.VMEM((LEV * HALF, 128), F32),
        pltpu.VMEM((LEV * HALF, 128), F32),
        pltpu.VMEM((2, LEV, HALF, 128), BF16),
        pltpu.VMEM((2, LEV, HALF, 128), BF16),
        pltpu.VMEM((HALF, 128), F32),
        pltpu.VMEM((2, ROWS, 128), F32),
        pltpu.VMEM((ROWS, NE), F32),
        dma((len(args),)), dma, dma((2,)), dma((2,)), dma((2, 3)), dma((2, 3)), dma((2, 3)), dma((2, 3)),
    ]
    any_spec = pl.BlockSpec(memory_space=pl.ANY)
    out = pl.pallas_call(
        kernel,
        out_shape=jax.ShapeDtypeStruct((ROWS, NE), F32),
        in_specs=[any_spec] * len(args),
        out_specs=any_spec,
        scratch_shapes=scratch,
        compiler_params=pltpu.CompilerParams(
            collective_id=0, has_side_effects=True, vmem_limit_bytes=60 * 2**20
        ),
        name="section",
    )(*args)
    return out.reshape(shape)


def solution(mesh):
    in_specs = (
        P("lev", None, "elem"), P("lev", None, "elem"), P("lev", None, "elem"), P("elem", None),
        P("elem"), P(), P(), P(), P(), P(),
    )
    out_specs = P("lev", None, "elem")
    return jax.shard_map(
        on_device, mesh=mesh, in_specs=in_specs, out_specs=out_specs, check_vma=False
    )
```

```python
import functools
import math

import jax
import jax.numpy as jnp
import numpy as np
from jax import lax
from jax.experimental import pallas as pl
from jax.experimental.pallas import tpu as pltpu
from jax.sharding import PartitionSpec as P

MESH = pl.DeviceIdType.MESH
F32 = jnp.float32
BF16 = jnp.bfloat16
LEV = 4
NL = 18
NODES = 16
ROWS = NL * NODES
NE = 512
HALF = ROWS // 2
LEVELS = NL * LEV
UNITS = 512
NT = (((1,), (1,)), ((), ()))


def derivative_table():
    nodes = [-1.0, -1.0 / math.sqrt(5.0), 1.0 / math.sqrt(5.0), 1.0]
    table = np.zeros((4, 4))
    for i in range(4):
        for j in range(4):
            if i == j:
                table[i, j] = sum(1.0 / (nodes[i] - nodes[m]) for m in range(4) if m != i)
            else:
                upper = lower = 1.0
                for m in range(4):
                    if m != i and m != j:
                        upper *= nodes[i] - nodes[m]
                    if m != j:
                        lower *= nodes[j] - nodes[m]
                table[i, j] = upper / lower
    return table


def derivative_blocks():
    table = derivative_table()
    eye4, eye9 = np.eye(4), np.eye(HALF // NODES)
    first = np.kron(table, eye4)
    second = np.kron(eye4, table)
    blocks = [0.05 * first, 0.05 * second, 0.005 * (first @ first + second @ second)]
    return np.concatenate([np.kron(eye9, b) for b in blocks]).astype(np.float32)


def kernel(
    t_hbm, u_hbm, v_hbm, pos_hbm, flag_hbm, d_hbm, w0_hbm, b0_hbm, wi_hbm, bi_hbm, wr_hbm,
    out_v,
    t_v, u_v, v_v, pos_v, flag_v, d_v, w0_v, b0_v, wi_v, bi_v, wr_v,
    q_s, tg_s, ag_s, dd_s, fl_s, w0_s, wi_s, bias_s,
    halo_s, halo_out, halo_in, col_s, col_out, col_in, x_s, h_s, heat_out, heat_in, hin_s, sum_s,
    in_sem, halo_send, halo_recv, col_send, col_recv, heat_send, heat_recv,
):
    me = lax.axis_index("lev")
    elem = lax.axis_index("elem")
    count = lax.axis_size("elem")
    nxt = lax.rem(elem + 1, count)
    prv = lax.rem(elem + count - 1, count)
    peers = [lax.rem(me + d, LEV) for d in (2, 1, 3)]

    loads = {}
    pairs = [
        ("pos", pos_hbm, pos_v), ("t", t_hbm, t_v), ("d", d_hbm, d_v), ("u", u_hbm, u_v),
        ("v", v_hbm, v_v), ("flag", flag_hbm, flag_v), ("w0", w0_hbm, w0_v), ("b0", b0_hbm, b0_v),
        ("bi", bi_hbm, bi_v), ("wi", wi_hbm, wi_v), ("wr", wr_hbm, wr_v),
    ]
    for n, (name, src, dst) in enumerate(pairs):
        loads[name] = pltpu.make_async_copy(src, dst, in_sem.at[n])
        loads[name].start()

    barrier = pltpu.get_barrier_semaphore()
    for p in peers:
        pl.semaphore_signal(barrier, inc=1, device_id=(elem, p), device_id_type=MESH)
    for e in (nxt, prv):
        pl.semaphore_signal(barrier, inc=1, device_id=(e, me), device_id_type=MESH)

    loads.pop("pos").wait()
    slot = lax.rem(pos_v[...] + 64, NE)
    for r in range(0, NE, 128):
        rows = lax.broadcasted_iota(jnp.int32, (128, NE), 0) + r
        q_s[pl.ds(r, 128), :] = jnp.where(rows == slot, 1.0, 0.0).astype(BF16)

    loads.pop("t").wait()
    loads.pop("flag").wait()
    flags = jnp.broadcast_to(flag_v[...].astype(F32), (16, NE)).astype(BF16)
    t_b = t_v[...].astype(BF16)
    both = lax.dot_general(
        jnp.concatenate([t_b, flags], axis=0), q_s[...], NT, preferred_element_type=F32
    )
    for c in range(4):
        ag_s[c] = both[:ROWS, 128 * c : 128 * c + 128]
    fl_s[...] = both[ROWS : ROWS + 8]

    loads.pop("d").wait()
    loads.pop("u").wait()
    loads.pop("v").wait()
    deriv = d_v[...].astype(BF16)
    parts = []
    for b in range(2):
        sl = slice(b * HALF, (b + 1) * HALF)
        g = jnp.dot(deriv, t_b[sl], preferred_element_type=F32)
        u = u_v[sl, :].astype(F32)
        v = v_v[sl, :].astype(F32)
        tend = g[2 * HALF :] - u * g[:HALF] - v * g[HALF : 2 * HALF]
        parts.append(tend.astype(BF16))
    tend = lax.dot_general(
        jnp.concatenate(parts, axis=0), q_s[...], NT, preferred_element_type=F32
    )
    for c in range(4):
        tg_s[c] = tend[:, 128 * c : 128 * c + 128]

    lane = lax.broadcasted_iota(jnp.int32, (NL, 128), 1)
    left = lane < 64
    inner = lane % 64

    def node(i, j, c):
        return tg_s[c, pl.ds(4 * i + j, NL, stride=NODES), :]

    halo_s[pl.ds(72, 8), :] = jnp.zeros((8, 128), F32)
    for j in range(4):
        halo_s[pl.ds(j, NL, stride=4), :] = jnp.where(left, node(3, j, 0), node(0, j, 0))
    halo_out[...] = halo_s[...].astype(BF16)
    pl.semaphore_wait(barrier, 5)
    halo_copies = []
    for n, e in enumerate((nxt, prv)):
        copy = pltpu.make_async_remote_copy(
            src_ref=halo_out, dst_ref=halo_in.at[n], send_sem=halo_send.at[n],
            recv_sem=halo_recv.at[n], device_id=(e, me), device_id_type=MESH,
        )
        copy.start()
        halo_copies.append(copy)

    def dss(c, halo):
        t = {(i, j): node(i, j, c) for i in range(4) for j in range(4)}
        for j in range(4):
            own0, own3 = t[0, j], t[3, j]
            near0, near3 = own0, own3
            if halo is not None:
                near3, near0 = halo[0][j], halo[1][j]
            after = pltpu.roll(jnp.where(left, node(0, j, (c + 1) % 4), near0), 64, 1)
            before = pltpu.roll(jnp.where(left, near3, node(3, j, (c + 3) % 4)), 64, 1)
            t[3, j] = (own3 + after) * 0.5
            t[0, j] = (own0 + before) * 0.5
        for i in range(4):
            own0, own3 = t[i, 0], t[i, 3]
            after = jnp.where(inner == 63, pltpu.roll(own0, 63, 1), pltpu.roll(own0, 127, 1))
            before = jnp.where(inner == 0, pltpu.roll(own3, 65, 1), pltpu.roll(own3, 1, 1))
            t[i, 3] = (own3 + after) * 0.5
            t[i, 0] = (own0 + before) * 0.5
        for i in range(4):
            for j in range(4):
                p = 4 * i + j
                dd_s[p, :NL, pl.ds(128 * c, 128)] = t[i, j]
                temp = ag_s[c, pl.ds(p, NL, stride=NODES), :]
                col_s[pl.ds(HALF * i + 72 * (c % 2) + j, NL, stride=4), :] = temp + t[i, j]

    col_copies = []

    def send_columns(s):
        col_out[s] = col_s[...].astype(BF16).reshape(LEV, HALF, 128)
        copies = []
        for n, p in enumerate(peers):
            copy = pltpu.make_async_remote_copy(
                src_ref=col_out.at[s, p], dst_ref=col_in.at[s, me], send_sem=col_send.at[s, n],
                recv_sem=col_recv.at[s, n], device_id=(elem, p), device_id_type=MESH,
            )
            copy.start()
            copies.append(copy)
        col_in[s, me] = col_out[s, me]
        col_copies.append(copies)

    dss(2, None)
    dss(3, None)
    send_columns(0)

    for copy in halo_copies:
        copy.wait_recv()
    from_before, from_after = [], []
    for n, store in enumerate((from_before, from_after)):
        halo_s[...] = halo_in[n].astype(F32)
        for j in range(4):
            store.append(halo_s[pl.ds(j, NL, stride=4), :])
    dss(0, (from_before, from_after))
    dss(1, None)
    send_columns(1)

    loads.pop("w0").wait()
    loads.pop("b0").wait()
    bias = b0_v[...] * 0.5
    coarse = bias.astype(BF16).astype(F32)
    row8 = lax.broadcasted_iota(jnp.int32, (8, UNITS), 0)
    tail = jnp.where(row8 == 0, coarse, jnp.where(row8 == 1, bias - coarse, 0.0))
    w0 = jnp.concatenate(
        [w0_v[...].astype(F32) * 0.5, tail, jnp.zeros((128 - LEVELS - 8, UNITS), F32)], axis=0
    )
    w0_s[...] = w0.T.astype(BF16)
    loads.pop("bi").wait()
    for m in range(2):
        bias_s[m] = jnp.broadcast_to(bi_v[pl.ds(m, 1), :] * 0.5, (128, UNITS)).T
    loads.pop("wi").wait()
    wi_s[...] = wi_v[...] * jnp.asarray(0.5, BF16)
    loads.pop("wr").wait()

    row8 = lax.broadcasted_iota(jnp.int32, (8, 1024), 0)
    ones = jnp.where(row8 < 2, 1.0, 0.0)

    def gate(h):
        return (h + h * jnp.tanh(h)).astype(BF16)

    heat_copies = []
    for s in range(2):
        for copy in col_copies[s]:
            copy.wait_recv()
        for src in range(LEV):
            block = col_in[s, src].astype(F32)
            for h in range(2):
                x_s[pl.ds(288 * h + 72 * src, 72), :] = block[72 * h : 72 * h + 72]

        x = jnp.concatenate(
            [x_s[pl.ds(288 * h + j, LEVELS, stride=4), :] for j in range(4) for h in range(2)], axis=1
        )
        x = jnp.concatenate([x, ones], axis=0).astype(BF16)
        hid = gate(jnp.dot(w0_s[:, : LEVELS + 8], x, preferred_element_type=F32))
        for m in range(2):
            pre = jnp.dot(wi_s[pl.ds(m * UNITS, UNITS), :], hid, preferred_element_type=F32)
            off = bias_s[m]
            hid = gate(pre + jnp.concatenate([off] * 8, axis=1))
        heat = jnp.dot(wr_v[...], hid, preferred_element_type=F32)
        for n in range(8):
            j, h = divmod(n, 2)
            h_s[pl.ds(288 * h + j, LEVELS, stride=4), :] = heat[:, 128 * n : 128 * n + 128]
        for dst in range(LEV):
            block = jnp.concatenate([h_s[pl.ds(288 * h + 72 * dst, 72), :] for h in range(2)], axis=0)
            heat_out[s, dst] = block.astype(BF16)
        copies = []
        for n, p in enumerate(peers):
            copy = pltpu.make_async_remote_copy(
                src_ref=heat_out.at[s, p], dst_ref=heat_in.at[s, me], send_sem=heat_send.at[s, n],
                recv_sem=heat_recv.at[s, n], device_id=(elem, p), device_id_type=MESH,
            )
            copy.start()
            copies.append(copy)
        heat_in[s, me] = heat_out[s, me]
        heat_copies.append(copies)

    for s in range(2):
        for copy in heat_copies[s]:
            copy.wait_recv()
        for q in range(LEV):
            hin_s[...] = heat_in[s, q].astype(F32)
            for h in range(2):
                c = 2 * (1 - s) + h
                lanes = pl.ds(128 * c, 128)
                day = fl_s[pl.ds(0, 1), lanes]
                for j in range(4):
                    p = 4 * q + j
                    heat = hin_s[pl.ds(72 * h + j, NL, stride=4), :]
                    sum_s[h, pl.ds(p, NL, stride=NODES), :] = dd_s[p, :NL, lanes] + heat * day
        lanes = pl.ds(256 * (1 - s), 256)
        total = jnp.concatenate([sum_s[0], sum_s[1]], axis=1).astype(BF16)
        back = jnp.dot(total, q_s[lanes, :], preferred_element_type=F32)
        if s == 0:
            out_v[...] = t_v[...] + back
        else:
            out_v[...] = out_v[...] + back

    for copy in halo_copies:
        copy.wait_send()
    for copies in col_copies + heat_copies:
        for copy in copies:
            copy.wait_send()


def on_device(t, u, v, pos, sunlit, w0, b0, wi, bi, wr):
    shape = t.shape
    args = [
        t.reshape(ROWS, NE), u.reshape(ROWS, NE), v.reshape(ROWS, NE), pos, sunlit.reshape(1, NE),
        jnp.asarray(derivative_blocks()), w0.T, b0.reshape(1, UNITS), wi.reshape(2 * UNITS, UNITS),
        bi, wr,
    ]
    vmem = [pltpu.VMEM(a.shape, a.dtype) for a in args]
    dma = pltpu.SemaphoreType.DMA
    scratch = vmem + [
        pltpu.VMEM((NE, NE), BF16),
        pltpu.VMEM((4, ROWS, 128), F32),
        pltpu.VMEM((4, ROWS, 128), F32),
        pltpu.VMEM((NODES, 24, NE), F32),
        pltpu.VMEM((8, NE), F32),
        pltpu.VMEM((UNITS, 128), BF16),
        pltpu.VMEM((2 * UNITS, UNITS), BF16),
        pltpu.VMEM((2, UNITS, 128), F32),
        pltpu.VMEM((80, 128), F32),
        pltpu.VMEM((80, 128), BF16),
        pltpu.VMEM((2, 80, 128), BF16),
        pltpu.VMEM((LEV * HALF, 128), F32),
        pltpu.VMEM((2, LEV, HALF, 128), BF16),
        pltpu.VMEM((2, LEV, HALF, 128), BF16),
        pltpu.VMEM((LEV * HALF, 128), F32),
        pltpu.VMEM((LEV * HALF, 128), F32),
        pltpu.VMEM((2, LEV, HALF, 128), BF16),
        pltpu.VMEM((2, LEV, HALF, 128), BF16),
        pltpu.VMEM((HALF, 128), F32),
        pltpu.VMEM((2, ROWS, 128), F32),
        dma((len(args),)), dma((2,)), dma((2,)), dma((2, 3)), dma((2, 3)), dma((2, 3)), dma((2, 3)),
    ]
    any_spec = pl.BlockSpec(memory_space=pltpu.HBM)
    out = pl.pallas_call(
        kernel,
        out_shape=pltpu.VMEM((ROWS, NE), F32),
        in_specs=[any_spec] * len(args),
        out_specs=pl.BlockSpec(memory_space=pltpu.VMEM),
        scratch_shapes=scratch,
        compiler_params=pltpu.CompilerParams(
            collective_id=0, has_side_effects=True, vmem_limit_bytes=60 * 2**20
        ),
        name="section",
    )(*args)
    return out.reshape(shape)


def solution(mesh):
    in_specs = (
        P("lev", None, "elem"), P("lev", None, "elem"), P("lev", None, "elem"), P("elem", None),
        P("elem"), P(), P(), P(), P(), P(),
    )
    out_specs = P("lev", None, "elem")
    return jax.shard_map(
        on_device, mesh=mesh, in_specs=in_specs, out_specs=out_specs, check_vma=False
    )
```

```python
import functools
import math

import jax
import jax.numpy as jnp
import numpy as np
from jax import lax
from jax.experimental import pallas as pl
from jax.experimental.pallas import tpu as pltpu
from jax.sharding import PartitionSpec as P

MESH = pl.DeviceIdType.MESH
F32 = jnp.float32
BF16 = jnp.bfloat16
LEV = 4
NL = 18
NODES = 16
ROWS = NL * NODES
NE = 512
BLOCK = 48
CHUNKS = (2, 3, 1, 0)
TALL = 80
SMALL = 32
LEVELS = NL * LEV
UNITS = 512
NT = (((1,), (1,)), ((), ()))


def derivative_table():
    nodes = [-1.0, -1.0 / math.sqrt(5.0), 1.0 / math.sqrt(5.0), 1.0]
    table = np.zeros((4, 4))
    for i in range(4):
        for j in range(4):
            if i == j:
                table[i, j] = sum(1.0 / (nodes[i] - nodes[m]) for m in range(4) if m != i)
            else:
                upper = lower = 1.0
                for m in range(4):
                    if m != i and m != j:
                        upper *= nodes[i] - nodes[m]
                    if m != j:
                        lower *= nodes[j] - nodes[m]
                table[i, j] = upper / lower
    return table


def derivative_blocks():
    table = derivative_table()
    eye4, eye_block = np.eye(4), np.eye(BLOCK // NODES)
    first = np.kron(table, eye4)
    second = np.kron(eye4, table)
    blocks = [0.05 * first, 0.05 * second, 0.005 * (first @ first + second @ second)]
    return np.concatenate([np.kron(eye_block, b) for b in blocks]).astype(np.float32)


def kernel(
    t_hbm, u_hbm, v_hbm, pos_hbm, flag_hbm, d_hbm, w0_hbm, b0_hbm, wi_hbm, bi_hbm, wr_hbm,
    out_v,
    t_v, u_v, v_v, pos_v, flag_v, d_v, w0_v, b0_v, wi_v, bi_v, wr_v,
    q_s, tg_s, ag_s, dd_s, fl_s, w0_s, wi_s, bias_s,
    small_s, halo_out, halo_in, pre_out, pre_in, late_out, late_in, col_s, x_s, h_s, hin_s, sum_s,
    col_out, col_in, heat_out, heat_in,
    in_sem, ready, halo_send, halo_recv, col_send, col_recv, heat_send, heat_recv,
    pre_send, pre_recv, late_send, late_recv,
):
    me = lax.axis_index("lev")
    elem = lax.axis_index("elem")
    count = lax.axis_size("elem")
    nxt = lax.rem(elem + 1, count)
    prv = lax.rem(elem + count - 1, count)
    peers = [lax.rem(me + d, LEV) for d in (2, 1, 3)]

    loads = {}
    pairs = [
        ("pos", pos_hbm, pos_v), ("t", t_hbm, t_v), ("d", d_hbm, d_v), ("u", u_hbm, u_v),
        ("v", v_hbm, v_v), ("flag", flag_hbm, flag_v), ("w0", w0_hbm, w0_v), ("b0", b0_hbm, b0_v),
        ("bi", bi_hbm, bi_v), ("wi", wi_hbm, wi_v), ("wr", wr_hbm, wr_v),
    ]
    for n, (name, src, dst) in enumerate(pairs):
        loads[name] = pltpu.make_async_copy(src, dst, in_sem.at[n])
        loads[name].start()

    barrier = pltpu.get_barrier_semaphore()
    for p in peers:
        pl.semaphore_signal(barrier, inc=1, device_id=(elem, p), device_id_type=MESH)
    for q in range(LEV):
        pl.semaphore_signal(barrier, inc=1, device_id=(prv, q), device_id_type=MESH)

    loads.pop("pos").wait()
    slot = lax.rem(pos_v[...] + 64, NE)
    for r in range(0, NE, 128):
        rows = lax.broadcasted_iota(jnp.int32, (128, NE), 0) + r
        q_s[pl.ds(r, 128), :] = jnp.where(rows == slot, 1.0, 0.0).astype(BF16)

    loads.pop("d").wait()
    deriv = d_v[...].astype(BF16)
    loads.pop("t").wait()
    t_hi = t_v[...].astype(BF16)
    loads.pop("u").wait()
    loads.pop("v").wait()
    parts = []
    for b in range(0, ROWS, BLOCK):
        sl = slice(b, b + BLOCK)
        g = jnp.dot(deriv, t_hi[sl], preferred_element_type=F32)
        u = u_v[sl, :].astype(F32)
        v = v_v[sl, :].astype(F32)
        tend = g[2 * BLOCK :] - u * g[:BLOCK] - v * g[BLOCK : 2 * BLOCK]
        parts.append(tend.astype(BF16))
    tend = jnp.concatenate(parts, axis=0)
    tg_s[0] = lax.dot_general(tend, q_s[:128, :], NT, preferred_element_type=F32)

    lane = lax.broadcasted_iota(jnp.int32, (NL, 128), 1)
    left = lane < 64
    inner = lane % 64

    def node(i, j, c):
        return tg_s[c, pl.ds(4 * i + j, NL, stride=NODES), :]

    def along_second(t, i):
        own0, own3 = t[i, 0], t[i, 3]
        after = jnp.where(inner == 63, pltpu.roll(own0, 63, 1), pltpu.roll(own0, 127, 1))
        before = jnp.where(inner == 0, pltpu.roll(own3, 65, 1), pltpu.roll(own3, 1, 1))
        t[i, 3] = (own3 + after) * 0.5
        t[i, 0] = (own0 + before) * 0.5

    edge = {(i, j): node(i, j, 0) for i in (0, 3) for j in range(4)}
    along_second(edge, 0)
    along_second(edge, 3)
    small_s[...] = jnp.zeros(small_s.shape, F32)
    for j in range(4):
        small_s[pl.ds(SMALL * j, NL), :] = jnp.where(left, edge[3, j], edge[0, j])
    halo_out[...] = small_s[...].astype(BF16).reshape(LEV, SMALL, 128)
    pl.semaphore_wait(barrier, 7)
    targets = [lax.rem(me + d, LEV) for d in range(LEV)]
    halo_copies = [
        [
            pltpu.make_async_remote_copy(
                src_ref=halo_out.at[q], dst_ref=halo_in.at[n, me], send_sem=halo_send.at[n, d],
                recv_sem=halo_recv.at[n, d], device_id=(e, q), device_id_type=MESH,
            )
            for d, q in enumerate(targets)
        ]
        for n, e in enumerate((nxt, prv))
    ]
    for copy in halo_copies[0]:
        copy.start()
    for q in targets:
        pl.semaphore_signal(ready, inc=1, device_id=(nxt, q), device_id_type=MESH)

    def send_back():
        pl.semaphore_wait(ready, LEV)
        for copy in halo_copies[1]:
            copy.start()

    rest = lax.dot_general(tend, q_s[128:, :], NT, preferred_element_type=F32)
    for c in range(1, 4):
        tg_s[c] = rest[:, 128 * (c - 1) : 128 * c]
    loads.pop("flag").wait()
    flags = jnp.broadcast_to(flag_v[...].astype(F32), (16, NE)).astype(BF16)
    t_lo = (t_v[...] - t_hi.astype(F32)).astype(BF16)
    both = lax.dot_general(
        jnp.concatenate([t_hi, t_lo, flags], axis=0), q_s[...], NT, preferred_element_type=F32
    )
    for c in range(4):
        lanes = slice(128 * c, 128 * c + 128)
        ag_s[c] = both[:ROWS, lanes] + both[ROWS : 2 * ROWS, lanes]
    fl_s[...] = both[2 * ROWS : 2 * ROWS + 8]

    def dss(part):
        c = CHUNKS[part]
        t = {(i, j): node(i, j, c) for i in range(4) for j in range(4)}
        for j in range(4):
            own0, own3 = t[0, j], t[3, j]
            near0, near3 = own0, own3
            if c == 0:
                near0 = near3 = jnp.zeros((NL, 128), F32)
            after = pltpu.roll(jnp.where(left, node(0, j, (c + 1) % 4), near0), 64, 1)
            before = pltpu.roll(jnp.where(left, near3, node(3, j, (c + 3) % 4)), 64, 1)
            t[3, j] = (own3 + after) * 0.5
            t[0, j] = (own0 + before) * 0.5
        for i in range(4):
            along_second(t, i)
        col = {}
        for i in range(4):
            for j in range(4):
                p = 4 * i + j
                dd_s[c, p, :NL, :] = t[i, j]
                col[i, j] = ag_s[c, pl.ds(p, NL, stride=NODES), :] + t[i, j]
                col_s[pl.ds(TALL * i + j, NL, stride=4), :] = col[i, j]
        return col

    def exchange(out, into, send, recv):
        copies = []
        for n, p in enumerate(peers):
            copy = pltpu.make_async_remote_copy(
                src_ref=out.at[p], dst_ref=into.at[me], send_sem=send.at[n],
                recv_sem=recv.at[n], device_id=(elem, p), device_id_type=MESH,
            )
            copy.start()
            copies.append(copy)
        into[me] = out[me]
        return copies

    def send_columns(part):
        for i in range(LEV):
            col_s[pl.ds(TALL * i + 72, 8), :] = jnp.zeros((8, 128), F32)
        col_out[part] = col_s[...].astype(BF16).reshape(LEV, TALL, 128)
        return exchange(
            col_out.at[part], col_in.at[part], col_send.at[part], col_recv.at[part]
        )

    def gate(h):
        return (h + h * jnp.tanh(h)).astype(BF16)

    def layers(x):
        width = x.shape[1]
        row8 = lax.broadcasted_iota(jnp.int32, (8, width), 0)
        x = jnp.concatenate([x, jnp.where(row8 < 2, 1.0, 0.0)], axis=0).astype(BF16)
        hid = gate(jnp.dot(w0_s[:, : LEVELS + 8], x, preferred_element_type=F32))
        for m in range(2):
            pre = jnp.dot(wi_s[pl.ds(m * UNITS, UNITS), :], hid, preferred_element_type=F32)
            hid = gate(pre + jnp.concatenate([bias_s[m]] * (width // 128), axis=1))
        return jnp.dot(wr_v[...], hid, preferred_element_type=F32)

    def network(part, copies):
        for copy in copies:
            copy.wait_recv()
        for src in range(LEV):
            x_s[pl.ds(72 * src, 72), :] = col_in[part, src].astype(F32)[:72]
        x = jnp.concatenate([x_s[pl.ds(j, LEVELS, stride=4), :] for j in range(4)], axis=1)
        heat = layers(x)
        for j in range(4):
            h_s[pl.ds(j, LEVELS, stride=4), :] = heat[:, 128 * j : 128 * j + 128]
        pad = jnp.zeros((8, 128), F32)
        for dst in range(LEV):
            block = jnp.concatenate([h_s[pl.ds(72 * dst, 72), :], pad], axis=0)
            heat_out[part, dst] = block.astype(BF16)
        return exchange(
            heat_out.at[part], heat_in.at[part], heat_send.at[part], heat_recv.at[part]
        )

    def unpack(part, late):
        c = CHUNKS[part]
        day = fl_s[pl.ds(0, 1), pl.ds(128 * c, 128)]
        for q in range(LEV):
            hin_s[...] = heat_in[part, q].astype(F32)
            for j in range(4):
                p = 4 * q + j
                heat = hin_s[pl.ds(j, NL, stride=4), :] * day
                if late is not None and q == 0:
                    heat = jnp.where(left, heat, late[j])
                if late is not None and q == 3:
                    heat = jnp.where(left, late[j], heat)
                sum_s[c, pl.ds(p, NL, stride=NODES), :] = dd_s[c, p, :NL, :] + heat

    def accumulate(first, last, base):
        total = jnp.concatenate([sum_s[c] for c in range(first, last)], axis=1).astype(BF16)
        rows = q_s[128 * first : 128 * last, :]
        out_v[...] = base[...] + jnp.dot(total, rows, preferred_element_type=F32)

    col_copies = []
    for part in range(4):
        col = dss(part)
        col_copies.append(send_columns(part))
    for j in range(4):
        small_s[pl.ds(SMALL * j, NL), :] = jnp.where(left, col[3, j], col[0, j])
    pre_out[...] = small_s[...].astype(BF16).reshape(LEV, SMALL, 128)
    pre_copies = exchange(pre_out, pre_in, pre_send, pre_recv)
    closing = lax.rem(elem, count // 2) == 0
    pl.when(jnp.logical_not(closing))(send_back)

    loads.pop("w0").wait()
    loads.pop("b0").wait()
    bias = b0_v[...] * 0.5
    coarse = bias.astype(BF16).astype(F32)
    row8 = lax.broadcasted_iota(jnp.int32, (8, UNITS), 0)
    tail = jnp.where(row8 == 0, coarse, jnp.where(row8 == 1, bias - coarse, 0.0))
    w0 = jnp.concatenate(
        [w0_v[...].astype(F32) * 0.5, tail, jnp.zeros((128 - LEVELS - 8, UNITS), F32)], axis=0
    )
    w0_s[...] = w0.T.astype(BF16)
    loads.pop("bi").wait()
    for m in range(2):
        bias_s[m] = jnp.broadcast_to(bi_v[pl.ds(m, 1), :] * 0.5, (128, UNITS)).T
    loads.pop("wi").wait()
    wi_s[...] = wi_v[...] * jnp.asarray(0.5, BF16)
    loads.pop("wr").wait()

    heat_copies = [network(part, col_copies[part]) for part in range(4)]
    pl.when(closing)(send_back)
    for copy in halo_copies[0] + halo_copies[1] + pre_copies:
        copy.wait_recv()
    added = []
    for src in range(LEV):
        edges = jnp.where(left, halo_in[0, src].astype(F32)[:NL], halo_in[1, src].astype(F32)[:NL])
        added.append(pltpu.roll(edges, 64, 1) * 0.5)
        x_s[pl.ds(NL * src, NL), :] = pre_in[src].astype(F32)[:NL] + added[src]
    h_s[:LEVELS, :] = layers(x_s[:LEVELS, :])
    day = fl_s[pl.ds(0, 1), pl.ds(0, 128)]
    for dst in range(LEV):
        small_s[pl.ds(SMALL * dst, NL), :] = added[dst] + h_s[pl.ds(NL * dst, NL), :] * day
    late_out[...] = small_s[...].astype(BF16).reshape(LEV, SMALL, 128)
    late_copies = exchange(late_out, late_in, late_send, late_recv)
    for part in range(4):
        for copy in heat_copies[part]:
            copy.wait_recv()
        if part < 3:
            unpack(part, None)
    accumulate(1, 4, t_v)
    for copy in late_copies:
        copy.wait_recv()
    unpack(3, [late_in[j].astype(F32)[:NL] for j in range(4)])
    accumulate(0, 1, out_v)

    for copies in halo_copies + col_copies + heat_copies + [pre_copies, late_copies]:
        for copy in copies:
            copy.wait_send()


def on_device(t, u, v, pos, sunlit, w0, b0, wi, bi, wr):
    shape = t.shape
    args = [
        t.reshape(ROWS, NE), u.reshape(ROWS, NE), v.reshape(ROWS, NE), pos, sunlit.reshape(1, NE),
        jnp.asarray(derivative_blocks()), w0.T, b0.reshape(1, UNITS), wi.reshape(2 * UNITS, UNITS),
        bi, wr,
    ]
    vmem = [pltpu.VMEM(a.shape, a.dtype) for a in args]
    dma = pltpu.SemaphoreType.DMA
    scratch = vmem + [
        pltpu.VMEM((NE, NE), BF16),
        pltpu.VMEM((4, ROWS, 128), F32),
        pltpu.VMEM((4, ROWS, 128), F32),
        pltpu.VMEM((4, NODES, 24, 128), F32),
        pltpu.VMEM((8, NE), F32),
        pltpu.VMEM((UNITS, 128), BF16),
        pltpu.VMEM((2 * UNITS, UNITS), BF16),
        pltpu.VMEM((2, UNITS, 128), F32),
        pltpu.VMEM((LEV * SMALL, 128), F32),
        pltpu.VMEM((LEV, SMALL, 128), BF16),
        pltpu.VMEM((2, LEV, SMALL, 128), BF16),
    ]
    scratch += [pltpu.VMEM((LEV, SMALL, 128), BF16)] * 4
    scratch += [
        pltpu.VMEM((LEV * TALL, 128), F32),
        pltpu.VMEM((ROWS, 128), F32),
        pltpu.VMEM((ROWS, 128), F32),
        pltpu.VMEM((TALL, 128), F32),
        pltpu.VMEM((4, ROWS, 128), F32),
    ]
    scratch += [pltpu.VMEM((4, LEV, TALL, 128), BF16)] * 4
    scratch += [
        dma((len(args),)), pltpu.SemaphoreType.REGULAR, dma((2, LEV)), dma((2, LEV)),
        dma((4, 3)), dma((4, 3)), dma((4, 3)), dma((4, 3)),
        dma((3,)), dma((3,)), dma((3,)), dma((3,)),
    ]
    any_spec = pl.BlockSpec(memory_space=pltpu.HBM)
    out = pl.pallas_call(
        kernel,
        out_shape=pltpu.VMEM((ROWS, NE), F32),
        in_specs=[any_spec] * len(args),
        out_specs=pl.BlockSpec(memory_space=pltpu.VMEM),
        scratch_shapes=scratch,
        compiler_params=pltpu.CompilerParams(
            collective_id=0, has_side_effects=True, vmem_limit_bytes=60 * 2**20
        ),
        name="section",
    )(*args)
    return out.reshape(shape)


def solution(mesh):
    in_specs = (
        P("lev", None, "elem"), P("lev", None, "elem"), P("lev", None, "elem"), P("elem", None),
        P("elem"), P(), P(), P(), P(), P(),
    )
    out_specs = P("lev", None, "elem")
    return jax.shard_map(
        on_device, mesh=mesh, in_specs=in_specs, out_specs=out_specs, check_vma=False
    )
```

```python
import functools
import math

import jax
import jax.numpy as jnp
import numpy as np
from jax import lax
from jax.experimental import pallas as pl
from jax.experimental.pallas import tpu as pltpu
from jax.sharding import PartitionSpec as P

MESH = pl.DeviceIdType.MESH
F32 = jnp.float32
BF16 = jnp.bfloat16
LEV = 4
NL = 18
NODES = 16
ROWS = NL * NODES
NE = 512
BLOCK = 48
PARTS = ((2,), (3, 1), (0,))
TALL = (80, 144, 80)
EDGE = 48
LEVELS = NL * LEV
UNITS = 512
NT = (((1,), (1,)), ((), ()))


def derivative_table():
    nodes = [-1.0, -1.0 / math.sqrt(5.0), 1.0 / math.sqrt(5.0), 1.0]
    table = np.zeros((4, 4))
    for i in range(4):
        for j in range(4):
            if i == j:
                table[i, j] = sum(1.0 / (nodes[i] - nodes[m]) for m in range(4) if m != i)
            else:
                upper = lower = 1.0
                for m in range(4):
                    if m != i and m != j:
                        upper *= nodes[i] - nodes[m]
                    if m != j:
                        lower *= nodes[j] - nodes[m]
                table[i, j] = upper / lower
    return table


def derivative_blocks():
    table = derivative_table()
    eye4, eye_block = np.eye(4), np.eye(BLOCK // NODES)
    first = np.kron(table, eye4)
    second = np.kron(eye4, table)
    blocks = [0.05 * first, 0.05 * second, 0.005 * (first @ first + second @ second)]
    return np.concatenate([np.kron(eye_block, b) for b in blocks]).astype(np.float32)


def kernel(
    t_hbm, u_hbm, v_hbm, pos_hbm, flag_hbm, d_hbm, w0_hbm, b0_hbm, wi_hbm, bi_hbm, wr_hbm,
    out_v,
    t_v, u_v, v_v, pos_v, flag_v, d_v, w0_v, b0_v, wi_v, bi_v, wr_v,
    q_s, tg_s, ag_s, dd_s, fl_s, w0_s, wi_s, bias_s,
    edge_s, halo_out, halo_in, pre_out, pre_in, add_s, col_s, x_s, h_s, hin_s, sum_s,
    col_out0, col_out1, col_out2, col_in0, col_in1, col_in2,
    heat_out0, heat_out1, heat_out2, heat_in0, heat_in1, heat_in2,
    in_sem, ready, halo_send, halo_recv, col_send, col_recv, heat_send, heat_recv,
    pre_send, pre_recv,
):
    col_out, col_in = (col_out0, col_out1, col_out2), (col_in0, col_in1, col_in2)
    heat_out, heat_in = (heat_out0, heat_out1, heat_out2), (heat_in0, heat_in1, heat_in2)
    me = lax.axis_index("lev")
    elem = lax.axis_index("elem")
    count = lax.axis_size("elem")
    nxt = lax.rem(elem + 1, count)
    prv = lax.rem(elem + count - 1, count)
    peers = [lax.rem(me + d, LEV) for d in (2, 1, 3)]

    loads = {}

    def start(first, pairs):
        for n, (name, src, dst) in enumerate(pairs):
            loads[name] = pltpu.make_async_copy(src, dst, in_sem.at[first + n])
            loads[name].start()

    start(0, [
        ("pos", pos_hbm, pos_v), ("t", t_hbm, t_v), ("u", u_hbm, u_v), ("v", v_hbm, v_v),
        ("d", d_hbm, d_v),
    ])

    barrier = pltpu.get_barrier_semaphore()
    for p in peers:
        pl.semaphore_signal(barrier, inc=1, device_id=(elem, p), device_id_type=MESH)
    for q in range(LEV):
        pl.semaphore_signal(barrier, inc=1, device_id=(prv, q), device_id_type=MESH)

    loads.pop("pos").wait()
    slot = lax.rem(pos_v[...] + 64, NE)
    for r in range(0, NE, 128):
        rows = lax.broadcasted_iota(jnp.int32, (128, NE), 0) + r
        q_s[pl.ds(r, 128), :] = jnp.where(rows == slot, 1.0, 0.0).astype(BF16)

    loads.pop("d").wait()
    deriv = d_v[...].astype(BF16)
    loads.pop("t").wait()
    t_hi = t_v[...].astype(BF16)
    loads.pop("u").wait()
    loads.pop("v").wait()
    parts = []
    for b in range(0, ROWS, BLOCK):
        sl = slice(b, b + BLOCK)
        g = jnp.dot(deriv, t_hi[sl], preferred_element_type=F32)
        u = u_v[sl, :].astype(F32)
        v = v_v[sl, :].astype(F32)
        tend = g[2 * BLOCK :] - u * g[:BLOCK] - v * g[BLOCK : 2 * BLOCK]
        parts.append(tend.astype(BF16))
    tend = jnp.concatenate(parts, axis=0)
    tg_s[0] = lax.dot_general(tend, q_s[:128, :], NT, preferred_element_type=F32)

    lane = lax.broadcasted_iota(jnp.int32, (NL, 128), 1)
    left = lane < 64
    inner = lane % 64

    def node(i, j, c):
        return tg_s[c, pl.ds(4 * i + j, NL, stride=NODES), :]

    def along_second(t, i):
        own0, own3 = t[i, 0], t[i, 3]
        after = jnp.where(inner == 63, pltpu.roll(own0, 63, 1), pltpu.roll(own0, 127, 1))
        before = jnp.where(inner == 0, pltpu.roll(own3, 65, 1), pltpu.roll(own3, 1, 1))
        t[i, 3] = (own3 + after) * 0.5
        t[i, 0] = (own0 + before) * 0.5

    edge = {(i, j): node(i, j, 0) for i in (0, 3) for j in range(4)}
    along_second(edge, 0)
    along_second(edge, 3)
    edge_s[...] = jnp.zeros(edge_s.shape, F32)
    for h in range(2):
        even, odd = 2 * h, 2 * h + 1
        edge_s[0, pl.ds(24 * h, NL), :] = jnp.where(left, edge[3, even], pltpu.roll(edge[3, odd], 64, 1))
        edge_s[1, pl.ds(24 * h, NL), :] = jnp.where(left, pltpu.roll(edge[0, even], 64, 1), edge[0, odd])
    halo_out[...] = edge_s[...].astype(BF16)
    pl.semaphore_wait(barrier, 7)
    targets = [lax.rem(me + d, LEV) for d in range(LEV)]
    halo_copies = [
        [
            pltpu.make_async_remote_copy(
                src_ref=halo_out.at[n], dst_ref=halo_in.at[n, me], send_sem=halo_send.at[n, d],
                recv_sem=halo_recv.at[n, d], device_id=(e, q), device_id_type=MESH,
            )
            for d, q in enumerate(targets)
        ]
        for n, e in enumerate((nxt, prv))
    ]
    for copy in halo_copies[0]:
        copy.start()
    for q in targets:
        pl.semaphore_signal(ready, inc=1, device_id=(nxt, q), device_id_type=MESH)

    start(5, [
        ("flag", flag_hbm, flag_v), ("w0", w0_hbm, w0_v), ("b0", b0_hbm, b0_v),
        ("bi", bi_hbm, bi_v), ("wi", wi_hbm, wi_v), ("wr", wr_hbm, wr_v),
    ])

    def send_back():
        pl.semaphore_wait(ready, LEV)
        for copy in halo_copies[1]:
            copy.start()

    rest = lax.dot_general(tend, q_s[128:, :], NT, preferred_element_type=F32)
    for c in range(1, 4):
        tg_s[c] = rest[:, 128 * (c - 1) : 128 * c]
    loads.pop("flag").wait()
    flags = jnp.broadcast_to(flag_v[...].astype(F32), (16, NE)).astype(BF16)
    t_lo = (t_v[...] - t_hi.astype(F32)).astype(BF16)
    stack = jnp.concatenate([t_hi, t_lo, flags], axis=0)

    def to_slots(first):
        both = lax.dot_general(
            stack, q_s[128 * first : 128 * first + 256, :], NT, preferred_element_type=F32
        )
        for h in range(2):
            lanes = slice(128 * h, 128 * h + 128)
            ag_s[first + h] = both[:ROWS, lanes] + both[ROWS : 2 * ROWS, lanes]
        fl_s[:, pl.ds(128 * first, 256)] = both[2 * ROWS : 2 * ROWS + 8]

    to_slots(2)

    def dss(part, h):
        c = PARTS[part][h]
        t = {(i, j): node(i, j, c) for i in range(4) for j in range(4)}
        for j in range(4):
            own0, own3 = t[0, j], t[3, j]
            near0, near3 = own0, own3
            if c == 0:
                near0 = near3 = jnp.zeros((NL, 128), F32)
            after = pltpu.roll(jnp.where(left, node(0, j, (c + 1) % 4), near0), 64, 1)
            before = pltpu.roll(jnp.where(left, near3, node(3, j, (c + 3) % 4)), 64, 1)
            t[3, j] = (own3 + after) * 0.5
            t[0, j] = (own0 + before) * 0.5
        for i in range(4):
            along_second(t, i)
        col = {}
        for i in range(4):
            for j in range(4):
                p = 4 * i + j
                dd_s[c, p, :NL, :] = t[i, j]
                col[i, j] = ag_s[c, pl.ds(p, NL, stride=NODES), :] + t[i, j]
                col_s[pl.ds(TALL[part] * i + 72 * h + j, NL, stride=4), :] = col[i, j]
        return col

    def exchange(out, into, send, recv):
        copies = []
        for n, p in enumerate(peers):
            copy = pltpu.make_async_remote_copy(
                src_ref=out.at[p], dst_ref=into.at[me], send_sem=send.at[n],
                recv_sem=recv.at[n], device_id=(elem, p), device_id_type=MESH,
            )
            copy.start()
            copies.append(copy)
        into[me] = out[me]
        return copies

    def send_columns(part):
        tall, used = TALL[part], 72 * len(PARTS[part])
        if tall > used:
            for i in range(LEV):
                col_s[pl.ds(tall * i + used, tall - used), :] = jnp.zeros((tall - used, 128), F32)
        col_out[part][...] = col_s[: LEV * tall, :].astype(BF16).reshape(LEV, tall, 128)
        return exchange(col_out[part], col_in[part], col_send.at[part], col_recv.at[part])

    def gate(h):
        return (h + h * jnp.tanh(h)).astype(BF16)

    def layers(x):
        width = x.shape[1]
        row8 = lax.broadcasted_iota(jnp.int32, (8, width), 0)
        x = jnp.concatenate([x, jnp.where(row8 < 2, 1.0, 0.0)], axis=0).astype(BF16)
        hid = gate(jnp.dot(w0_s[:, : LEVELS + 8], x, preferred_element_type=F32))
        for m in range(2):
            pre = jnp.dot(wi_s[pl.ds(m * UNITS, UNITS), :], hid, preferred_element_type=F32)
            hid = gate(pre + jnp.concatenate([bias_s[m]] * (width // 128), axis=1))
        return jnp.dot(wr_v[...], hid, preferred_element_type=F32)

    def network(part, copies):
        size = len(PARTS[part])
        for copy in copies:
            copy.wait_recv()
        for src in range(LEV):
            block = col_in[part][src].astype(F32)
            for h in range(size):
                x_s[pl.ds(288 * h + 72 * src, 72), :] = block[72 * h : 72 * h + 72]
        heat = layers(jnp.concatenate(
            [x_s[pl.ds(288 * h + j, LEVELS, stride=4), :] for j in range(4) for h in range(size)], axis=1
        ))
        for n in range(4 * size):
            j, h = divmod(n, size)
            h_s[pl.ds(288 * h + j, LEVELS, stride=4), :] = heat[:, 128 * n : 128 * n + 128]
        for dst in range(LEV):
            block = [h_s[pl.ds(288 * h + 72 * dst, 72), :] for h in range(size)]
            if size == 1:
                block.append(jnp.zeros((8, 128), F32))
            heat_out[part][dst] = jnp.concatenate(block, axis=0).astype(BF16)
        return exchange(heat_out[part], heat_in[part], heat_send.at[part], heat_recv.at[part])

    def unpack(part, late):
        for q in range(LEV):
            hin_s[: TALL[part], :] = heat_in[part][q].astype(F32)
            for h, c in enumerate(PARTS[part]):
                day = fl_s[pl.ds(0, 1), pl.ds(128 * c, 128)]
                for j in range(4):
                    p = 4 * q + j
                    heat = hin_s[pl.ds(72 * h + j, NL, stride=4), :] * day
                    if c == 0 and q == 0:
                        heat = jnp.where(left, heat, late[j])
                    if c == 0 and q == 3:
                        heat = jnp.where(left, late[j], heat)
                    sum_s[c, pl.ds(p, NL, stride=NODES), :] = dd_s[c, p, :NL, :] + heat

    col_copies = []
    for part, chunks in enumerate(PARTS):
        for h in range(len(chunks)):
            col = dss(part, h)
        col_copies.append(send_columns(part))
        if part == 0:
            to_slots(0)
    col_s[pl.ds(72, 8), :] = jnp.zeros((8, 128), F32)
    for j in range(4):
        col_s[pl.ds(j, NL, stride=4), :] = jnp.where(left, col[3, j], col[0, j])
    pre_out[...] = col_s[:80, :].astype(BF16)
    pre_copies = []
    for n, p in enumerate(peers):
        copy = pltpu.make_async_remote_copy(
            src_ref=pre_out, dst_ref=pre_in.at[me], send_sem=pre_send.at[n],
            recv_sem=pre_recv.at[n], device_id=(elem, p), device_id_type=MESH,
        )
        copy.start()
        pre_copies.append(copy)
    pre_in[me] = pre_out[...]
    closing = lax.rem(elem, count // 2) == 0
    pl.when(jnp.logical_not(closing))(send_back)

    loads.pop("w0").wait()
    loads.pop("b0").wait()
    bias = b0_v[...] * 0.5
    coarse = bias.astype(BF16).astype(F32)
    row8 = lax.broadcasted_iota(jnp.int32, (8, UNITS), 0)
    tail = jnp.where(row8 == 0, coarse, jnp.where(row8 == 1, bias - coarse, 0.0))
    w0 = jnp.concatenate(
        [w0_v[...].astype(F32) * 0.5, tail, jnp.zeros((128 - LEVELS - 8, UNITS), F32)], axis=0
    )
    w0_s[...] = w0.T.astype(BF16)
    loads.pop("bi").wait()
    for m in range(2):
        bias_s[m] = jnp.broadcast_to(bi_v[pl.ds(m, 1), :] * 0.5, (128, UNITS)).T
    loads.pop("wi").wait()
    wi_s[...] = wi_v[...] * jnp.asarray(0.5, BF16)
    loads.pop("wr").wait()

    heat_copies = [network(part, copies) for part, copies in enumerate(col_copies)]

    pl.when(closing)(send_back)
    for copy in pre_copies:
        copy.wait_recv()
    for src in range(LEV):
        x_s[pl.ds(72 * src, 72), :] = pre_in[src].astype(F32)[:72]
    for copy in halo_copies[0] + halo_copies[1]:
        copy.wait_recv()
    for src in range(LEV):
        below, above = halo_in[0, src].astype(F32), halo_in[1, src].astype(F32)
        for j in range(4):
            row = 24 * (j // 2)
            before, after = below[row : row + NL], above[row : row + NL]
            if j % 2 == 0:
                before = pltpu.roll(before, 64, 1)
            else:
                after = pltpu.roll(after, 64, 1)
            rows = pl.ds(72 * src + j, NL, stride=4)
            add = jnp.where(left, after, before) * 0.5
            add_s[rows, :] = add
            x_s[rows, :] = x_s[rows, :] + add
    heat = layers(
        jnp.concatenate([x_s[pl.ds(j, LEVELS, stride=4), :] for j in range(4)], axis=1)
    )
    for j in range(4):
        h_s[pl.ds(j, LEVELS, stride=4), :] = heat[:, 128 * j : 128 * j + 128]
    day = fl_s[pl.ds(0, 1), pl.ds(0, 128)]
    late = []
    for j in range(4):
        rows = pl.ds(72 * me + j, NL, stride=4)
        late.append(add_s[rows, :] + h_s[rows, :] * day)
    for part in range(len(PARTS)):
        for copy in heat_copies[part]:
            copy.wait_recv()
        unpack(part, late)
    total = jnp.concatenate([sum_s[c] for c in range(4)], axis=1).astype(BF16)
    out_v[...] = t_v[...] + jnp.dot(total, q_s[...], preferred_element_type=F32)

    for copies in halo_copies + col_copies + heat_copies + [pre_copies]:
        for copy in copies:
            copy.wait_send()


def on_device(t, u, v, pos, sunlit, w0, b0, wi, bi, wr):
    shape = t.shape
    args = [
        t.reshape(ROWS, NE), u.reshape(ROWS, NE), v.reshape(ROWS, NE), pos, sunlit.reshape(1, NE),
        jnp.asarray(derivative_blocks()), w0.T, b0.reshape(1, UNITS), wi.reshape(2 * UNITS, UNITS),
        bi, wr,
    ]
    vmem = [pltpu.VMEM(a.shape, a.dtype) for a in args]
    dma = pltpu.SemaphoreType.DMA
    scratch = vmem + [
        pltpu.VMEM((NE, NE), BF16),
        pltpu.VMEM((4, ROWS, 128), F32),
        pltpu.VMEM((4, ROWS, 128), F32),
        pltpu.VMEM((4, NODES, 24, 128), F32),
        pltpu.VMEM((8, NE), F32),
        pltpu.VMEM((UNITS, 128), BF16),
        pltpu.VMEM((2 * UNITS, UNITS), BF16),
        pltpu.VMEM((2, UNITS, 128), F32),
        pltpu.VMEM((2, EDGE, 128), F32),
        pltpu.VMEM((2, EDGE, 128), BF16),
        pltpu.VMEM((2, LEV, EDGE, 128), BF16),
        pltpu.VMEM((80, 128), BF16),
        pltpu.VMEM((LEV, 80, 128), BF16),
        pltpu.VMEM((ROWS, 128), F32),
        pltpu.VMEM((LEV * max(TALL), 128), F32),
        pltpu.VMEM((2 * ROWS, 128), F32),
        pltpu.VMEM((2 * ROWS, 128), F32),
        pltpu.VMEM((max(TALL), 128), F32),
        pltpu.VMEM((4, ROWS, 128), F32),
    ]
    scratch += [pltpu.VMEM((LEV, tall, 128), BF16) for _ in range(4) for tall in TALL]
    scratch += [
        dma((len(args),)), pltpu.SemaphoreType.REGULAR, dma((2, LEV)), dma((2, LEV)),
        dma((3, 3)), dma((3, 3)), dma((3, 3)), dma((3, 3)), dma((3,)), dma((3,)),
    ]
    any_spec = pl.BlockSpec(memory_space=pltpu.HBM)
    out = pl.pallas_call(
        kernel,
        out_shape=pltpu.VMEM((ROWS, NE), F32),
        in_specs=[any_spec] * len(args),
        out_specs=pl.BlockSpec(memory_space=pltpu.VMEM),
        scratch_shapes=scratch,
        compiler_params=pltpu.CompilerParams(
            collective_id=0, has_side_effects=True, vmem_limit_bytes=60 * 2**20
        ),
        name="section",
    )(*args)
    return out.reshape(shape)


def solution(mesh):
    in_specs = (
        P("lev", None, "elem"), P("lev", None, "elem"), P("lev", None, "elem"), P("elem", None),
        P("elem"), P(), P(), P(), P(), P(),
    )
    out_specs = P("lev", None, "elem")
    return jax.shard_map(
        on_device, mesh=mesh, in_specs=in_specs, out_specs=out_specs, check_vma=False
    )
```

```python
import functools
import math

import jax
import jax.numpy as jnp
import numpy as np
from jax import lax
from jax.experimental import pallas as pl
from jax.experimental.pallas import tpu as pltpu
from jax.sharding import PartitionSpec as P

MESH = pl.DeviceIdType.MESH
F32 = jnp.float32
BF16 = jnp.bfloat16
LEV = 4
NL = 18
NODES = 16
ROWS = NL * NODES
NE = 512
BLOCK = 48
TALLER = 24 * NODES
PARTS = ((2,), (3, 1), (0,))
TALL = (80, 144, 80)
EDGE = 48
LEVELS = NL * LEV
UNITS = 512
NT = (((1,), (1,)), ((), ()))


def derivative_table():
    nodes = [-1.0, -1.0 / math.sqrt(5.0), 1.0 / math.sqrt(5.0), 1.0]
    table = np.zeros((4, 4))
    for i in range(4):
        for j in range(4):
            if i == j:
                table[i, j] = sum(1.0 / (nodes[i] - nodes[m]) for m in range(4) if m != i)
            else:
                upper = lower = 1.0
                for m in range(4):
                    if m != i and m != j:
                        upper *= nodes[i] - nodes[m]
                    if m != j:
                        lower *= nodes[j] - nodes[m]
                table[i, j] = upper / lower
    return table


def derivative_blocks():
    table = derivative_table()
    eye4, eye_block = np.eye(4), np.eye(BLOCK // NODES)
    first = np.kron(table, eye4)
    second = np.kron(eye4, table)
    blocks = [0.05 * first, 0.05 * second, 0.005 * (first @ first + second @ second)]
    return np.concatenate([np.kron(eye_block, b) for b in blocks]).astype(np.float32)


def kernel(
    t_hbm, u_hbm, v_hbm, pos_hbm, flag_hbm, d_hbm, w0_hbm, b0_hbm, wi_hbm, bi_hbm, wr_hbm,
    out_v,
    t_v, u_v, v_v, pos_v, flag_v, d_v, w0_v, b0_v, wi_v, bi_v, wr_v,
    q_s, tg_s, ag_s, dd_s, fl_s, w0_s, wi_s, bias_s,
    edge_s, halo_out, halo_in, pre_out, pre_in, add_s, col_s, x_s, h_s, hin_s, sum_s,
    col_out0, col_out1, col_out2, col_in0, col_in1, col_in2,
    heat_out0, heat_out1, heat_out2, heat_in0, heat_in1, heat_in2,
    in_sem, ready, halo_send, halo_recv, col_send, col_recv, heat_send, heat_recv,
    pre_send, pre_recv,
):
    col_out, col_in = (col_out0, col_out1, col_out2), (col_in0, col_in1, col_in2)
    heat_out, heat_in = (heat_out0, heat_out1, heat_out2), (heat_in0, heat_in1, heat_in2)
    me = lax.axis_index("lev")
    elem = lax.axis_index("elem")
    count = lax.axis_size("elem")
    nxt = lax.rem(elem + 1, count)
    prv = lax.rem(elem + count - 1, count)
    peers = [lax.rem(me + d, LEV) for d in (2, 1, 3)]

    loads = {}

    def start(first, pairs):
        for n, (name, src, dst) in enumerate(pairs):
            loads[name] = pltpu.make_async_copy(src, dst, in_sem.at[first + n])
            loads[name].start()

    start(0, [
        ("pos", pos_hbm, pos_v), ("t", t_hbm, t_v), ("u", u_hbm, u_v), ("v", v_hbm, v_v),
        ("d", d_hbm, d_v), ("flag", flag_hbm, flag_v),
    ])

    barrier = pltpu.get_barrier_semaphore()
    for p in peers:
        pl.semaphore_signal(barrier, inc=1, device_id=(elem, p), device_id_type=MESH)
    for q in range(LEV):
        pl.semaphore_signal(barrier, inc=1, device_id=(prv, q), device_id_type=MESH)

    loads.pop("pos").wait()
    slot = lax.rem(pos_v[...] + 64, NE)
    for r in range(0, NE, 128):
        rows = lax.broadcasted_iota(jnp.int32, (128, NE), 0) + r
        q_s[pl.ds(r, 128), :] = jnp.where(rows == slot, 1.0, 0.0).astype(BF16)

    loads.pop("d").wait()
    deriv = d_v[...].astype(BF16)
    loads.pop("t").wait()
    t_hi = t_v[...].astype(BF16)
    loads.pop("u").wait()
    loads.pop("v").wait()
    parts = []
    for b in range(0, ROWS, BLOCK):
        sl = slice(b, b + BLOCK)
        g = jnp.dot(deriv, t_hi[sl], preferred_element_type=F32)
        u = u_v[sl, :].astype(F32)
        v = v_v[sl, :].astype(F32)
        tend = g[2 * BLOCK :] - u * g[:BLOCK] - v * g[BLOCK : 2 * BLOCK]
        parts.append(tend.astype(BF16))
    tend = jnp.concatenate(parts, axis=0)
    tg_s[0, :ROWS] = lax.dot_general(tend, q_s[:128, :], NT, preferred_element_type=F32)

    lane = lax.broadcasted_iota(jnp.int32, (NL, 128), 1)
    left = lane < 64
    inner = lane % 64

    def node(i, j, c):
        return tg_s[c, pl.ds(4 * i + j, NL, stride=NODES), :]

    def along_second(t, i):
        own0, own3 = t[i, 0], t[i, 3]
        after = jnp.where(inner == 63, pltpu.roll(own0, 63, 1), pltpu.roll(own0, 127, 1))
        before = jnp.where(inner == 0, pltpu.roll(own3, 65, 1), pltpu.roll(own3, 1, 1))
        t[i, 3] = (own3 + after) * 0.5
        t[i, 0] = (own0 + before) * 0.5

    edge = {(i, j): node(i, j, 0) for i in (0, 3) for j in range(4)}
    along_second(edge, 0)
    along_second(edge, 3)
    edge_s[...] = jnp.zeros(edge_s.shape, F32)
    for h in range(2):
        even, odd = 2 * h, 2 * h + 1
        edge_s[0, pl.ds(24 * h, NL), :] = jnp.where(left, edge[3, even], pltpu.roll(edge[3, odd], 64, 1))
        edge_s[1, pl.ds(24 * h, NL), :] = jnp.where(left, pltpu.roll(edge[0, even], 64, 1), edge[0, odd])
    halo_out[...] = edge_s[...].astype(BF16)
    pl.semaphore_wait(barrier, 7)
    targets = [lax.rem(me + d, LEV) for d in range(LEV)]
    halo_copies = [
        [
            pltpu.make_async_remote_copy(
                src_ref=halo_out.at[n], dst_ref=halo_in.at[n, me], send_sem=halo_send.at[n, d],
                recv_sem=halo_recv.at[n, d], device_id=(e, q), device_id_type=MESH,
            )
            for d, q in enumerate(targets)
        ]
        for n, e in enumerate((nxt, prv))
    ]
    for copy in halo_copies[0]:
        copy.start()


    def send_back():
        pl.semaphore_wait(ready, LEV)
        for copy in halo_copies[1]:
            copy.start()

    rest = lax.dot_general(tend, q_s[128:, :], NT, preferred_element_type=F32)
    for c in range(1, 4):
        tg_s[c, :ROWS] = rest[:, 128 * (c - 1) : 128 * c]
    loads.pop("flag").wait()
    flags = jnp.broadcast_to(flag_v[...].astype(F32), (16, NE)).astype(BF16)
    t_lo = (t_v[...] - t_hi.astype(F32)).astype(BF16)
    stack = jnp.concatenate([t_hi, t_lo, flags], axis=0)

    def to_slots(first):
        both = lax.dot_general(
            stack, q_s[128 * first : 128 * first + 256, :], NT, preferred_element_type=F32
        )
        for h in range(2):
            lanes = slice(128 * h, 128 * h + 128)
            ag_s[first + h, :ROWS] = both[:ROWS, lanes] + both[ROWS : 2 * ROWS, lanes]
        fl_s[:, pl.ds(128 * first, 256)] = both[2 * ROWS : 2 * ROWS + 8]

    to_slots(2)

    def dss(part, h):
        c = PARTS[part][h]
        t = {(i, j): node(i, j, c) for i in range(4) for j in range(4)}
        for j in range(4):
            own0, own3 = t[0, j], t[3, j]
            near0, near3 = own0, own3
            if c == 0:
                near0 = near3 = jnp.zeros((NL, 128), F32)
            after = pltpu.roll(jnp.where(left, node(0, j, (c + 1) % 4), near0), 64, 1)
            before = pltpu.roll(jnp.where(left, near3, node(3, j, (c + 3) % 4)), 64, 1)
            t[3, j] = (own3 + after) * 0.5
            t[0, j] = (own0 + before) * 0.5
        for i in range(4):
            along_second(t, i)
        col = {}
        for i in range(4):
            for j in range(4):
                p = 4 * i + j
                dd_s[c, p, :NL, :] = t[i, j]
                col[i, j] = ag_s[c, pl.ds(p, NL, stride=NODES), :] + t[i, j]
                col_s[pl.ds(TALL[part] * i + 72 * h + j, NL, stride=4), :] = col[i, j]
        return col

    def exchange(out, into, send, recv):
        copies = []
        for n, p in enumerate(peers):
            copy = pltpu.make_async_remote_copy(
                src_ref=out.at[p], dst_ref=into.at[me], send_sem=send.at[n],
                recv_sem=recv.at[n], device_id=(elem, p), device_id_type=MESH,
            )
            copy.start()
            copies.append(copy)
        into[me] = out[me]
        return copies

    def send_columns(part):
        tall, used = TALL[part], 72 * len(PARTS[part])
        if tall > used:
            for i in range(LEV):
                col_s[pl.ds(tall * i + used, tall - used), :] = jnp.zeros((tall - used, 128), F32)
        col_out[part][...] = col_s[: LEV * tall, :].astype(BF16).reshape(LEV, tall, 128)
        return exchange(col_out[part], col_in[part], col_send.at[part], col_recv.at[part])

    def gate(h):
        return (h + h * jnp.tanh(h)).astype(BF16)

    def layers(x):
        width = x.shape[1]
        row8 = lax.broadcasted_iota(jnp.int32, (8, width), 0)
        x = jnp.concatenate([x, jnp.where(row8 < 2, 1.0, 0.0)], axis=0).astype(BF16)
        hid = gate(jnp.dot(w0_s[:, : LEVELS + 8], x, preferred_element_type=F32))
        for m in range(2):
            pre = jnp.dot(wi_s[pl.ds(m * UNITS, UNITS), :], hid, preferred_element_type=F32)
            hid = gate(pre + jnp.concatenate([bias_s[m]] * (width // 128), axis=1))
        return jnp.dot(wr_v[...], hid, preferred_element_type=F32)

    def network(part, copies):
        size = len(PARTS[part])
        for copy in copies:
            copy.wait_recv()
        for src in range(LEV):
            block = col_in[part][src].astype(F32)
            for h in range(size):
                x_s[pl.ds(288 * h + 72 * src, 72), :] = block[72 * h : 72 * h + 72]
        heat = layers(jnp.concatenate(
            [x_s[pl.ds(288 * h + j, LEVELS, stride=4), :] for j in range(4) for h in range(size)], axis=1
        ))
        for n in range(4 * size):
            j, h = divmod(n, size)
            h_s[pl.ds(288 * h + j, LEVELS, stride=4), :] = heat[:, 128 * n : 128 * n + 128]
        for dst in range(LEV):
            block = [h_s[pl.ds(288 * h + 72 * dst, 72), :] for h in range(size)]
            if size == 1:
                block.append(jnp.zeros((8, 128), F32))
            heat_out[part][dst] = jnp.concatenate(block, axis=0).astype(BF16)
        return exchange(heat_out[part], heat_in[part], heat_send.at[part], heat_recv.at[part])

    def unpack(part, late):
        for q in range(LEV):
            hin_s[: TALL[part], :] = heat_in[part][q].astype(F32)
            for h, c in enumerate(PARTS[part]):
                day = fl_s[pl.ds(0, 1), pl.ds(128 * c, 128)]
                for j in range(4):
                    p = 4 * q + j
                    heat = hin_s[pl.ds(72 * h + j, NL, stride=4), :] * day
                    if c == 0 and q == 0:
                        heat = jnp.where(left, heat, late[j])
                    if c == 0 and q == 3:
                        heat = jnp.where(left, late[j], heat)
                    sum_s[c, pl.ds(p, NL, stride=NODES), :] = dd_s[c, p, :NL, :] + heat

    col_copies = []
    for part, chunks in enumerate(PARTS):
        for h in range(len(chunks)):
            col = dss(part, h)
        col_copies.append(send_columns(part))
        if part == 0:
            start(6, [
                ("w0", w0_hbm, w0_v), ("b0", b0_hbm, b0_v), ("bi", bi_hbm, bi_v),
                ("wi", wi_hbm, wi_v), ("wr", wr_hbm, wr_v),
            ])
            for q in targets:
                pl.semaphore_signal(ready, inc=1, device_id=(nxt, q), device_id_type=MESH)
            to_slots(0)
    col_s[pl.ds(72, 8), :] = jnp.zeros((8, 128), F32)
    for j in range(4):
        col_s[pl.ds(j, NL, stride=4), :] = jnp.where(left, col[3, j], col[0, j])
    pre_out[...] = col_s[:80, :].astype(BF16)
    pre_copies = []
    for n, p in enumerate(peers):
        copy = pltpu.make_async_remote_copy(
            src_ref=pre_out, dst_ref=pre_in.at[me], send_sem=pre_send.at[n],
            recv_sem=pre_recv.at[n], device_id=(elem, p), device_id_type=MESH,
        )
        copy.start()
        pre_copies.append(copy)
    pre_in[me] = pre_out[...]
    closing = lax.rem(elem, count // 2) == 0

    loads.pop("w0").wait()
    loads.pop("b0").wait()
    bias = b0_v[...] * 0.5
    coarse = bias.astype(BF16).astype(F32)
    row8 = lax.broadcasted_iota(jnp.int32, (8, UNITS), 0)
    tail = jnp.where(row8 == 0, coarse, jnp.where(row8 == 1, bias - coarse, 0.0))
    w0 = jnp.concatenate(
        [w0_v[...].astype(F32) * 0.5, tail, jnp.zeros((128 - LEVELS - 8, UNITS), F32)], axis=0
    )
    w0_s[...] = w0.T.astype(BF16)
    loads.pop("bi").wait()
    for m in range(2):
        bias_s[m] = jnp.broadcast_to(bi_v[pl.ds(m, 1), :] * 0.5, (128, UNITS)).T
    loads.pop("wi").wait()
    wi_s[...] = wi_v[...] * jnp.asarray(0.5, BF16)
    loads.pop("wr").wait()

    pl.when(jnp.logical_not(closing))(send_back)
    heat_copies = [network(part, copies) for part, copies in enumerate(col_copies)]

    pl.when(closing)(send_back)
    for copy in pre_copies:
        copy.wait_recv()
    for src in range(LEV):
        x_s[pl.ds(72 * src, 72), :] = pre_in[src].astype(F32)[:72]
    for copy in halo_copies[0] + halo_copies[1]:
        copy.wait_recv()
    for src in range(LEV):
        below, above = halo_in[0, src].astype(F32), halo_in[1, src].astype(F32)
        for j in range(4):
            row = 24 * (j // 2)
            before, after = below[row : row + NL], above[row : row + NL]
            if j % 2 == 0:
                before = pltpu.roll(before, 64, 1)
            else:
                after = pltpu.roll(after, 64, 1)
            rows = pl.ds(72 * src + j, NL, stride=4)
            add = jnp.where(left, after, before) * 0.5
            add_s[rows, :] = add
            x_s[rows, :] = x_s[rows, :] + add
    heat = layers(
        jnp.concatenate([x_s[pl.ds(j, LEVELS, stride=4), :] for j in range(4)], axis=1)
    )
    for j in range(4):
        h_s[pl.ds(j, LEVELS, stride=4), :] = heat[:, 128 * j : 128 * j + 128]
    day = fl_s[pl.ds(0, 1), pl.ds(0, 128)]
    late = []
    for j in range(4):
        rows = pl.ds(72 * me + j, NL, stride=4)
        late.append(add_s[rows, :] + h_s[rows, :] * day)
    def accumulate(first, last, base):
        total = jnp.concatenate([sum_s[c, :ROWS] for c in range(first, last)], axis=1).astype(BF16)
        rows = q_s[128 * first : 128 * last, :]
        out_v[...] = base[...] + jnp.dot(total, rows, preferred_element_type=F32)

    for part in range(len(PARTS)):
        for copy in heat_copies[part]:
            copy.wait_recv()
        unpack(part, late)
        if part == 1:
            accumulate(1, 4, t_v)
    accumulate(0, 1, out_v)

    for copies in halo_copies + col_copies + heat_copies + [pre_copies]:
        for copy in copies:
            copy.wait_send()


def on_device(t, u, v, pos, sunlit, w0, b0, wi, bi, wr):
    shape = t.shape
    args = [
        t.reshape(ROWS, NE), u.reshape(ROWS, NE), v.reshape(ROWS, NE), pos, sunlit.reshape(1, NE),
        jnp.asarray(derivative_blocks()), w0.T, b0.reshape(1, UNITS), wi.reshape(2 * UNITS, UNITS),
        bi, wr,
    ]
    vmem = [pltpu.VMEM(a.shape, a.dtype) for a in args]
    dma = pltpu.SemaphoreType.DMA
    scratch = vmem + [
        pltpu.VMEM((NE, NE), BF16),
        pltpu.VMEM((4, TALLER, 128), F32),
        pltpu.VMEM((4, TALLER, 128), F32),
        pltpu.VMEM((4, NODES, 24, 128), F32),
        pltpu.VMEM((8, NE), F32),
        pltpu.VMEM((UNITS, 128), BF16),
        pltpu.VMEM((2 * UNITS, UNITS), BF16),
        pltpu.VMEM((2, UNITS, 128), F32),
        pltpu.VMEM((2, EDGE, 128), F32),
        pltpu.VMEM((2, EDGE, 128), BF16),
        pltpu.VMEM((2, LEV, EDGE, 128), BF16),
        pltpu.VMEM((80, 128), BF16),
        pltpu.VMEM((LEV, 80, 128), BF16),
        pltpu.VMEM((ROWS + 32, 128), F32),
        pltpu.VMEM((LEV * max(TALL) + 32, 128), F32),
        pltpu.VMEM((2 * ROWS + 32, 128), F32),
        pltpu.VMEM((2 * ROWS + 32, 128), F32),
        pltpu.VMEM((max(TALL) + 32, 128), F32),
        pltpu.VMEM((4, TALLER, 128), F32),
    ]
    scratch += [pltpu.VMEM((LEV, tall, 128), BF16) for _ in range(4) for tall in TALL]
    scratch += [
        dma((len(args),)), pltpu.SemaphoreType.REGULAR, dma((2, LEV)), dma((2, LEV)),
        dma((3, 3)), dma((3, 3)), dma((3, 3)), dma((3, 3)), dma((3,)), dma((3,)),
    ]
    any_spec = pl.BlockSpec(memory_space=pltpu.HBM)
    out = pl.pallas_call(
        kernel,
        out_shape=pltpu.VMEM((ROWS, NE), F32),
        in_specs=[any_spec] * len(args),
        out_specs=pl.BlockSpec(memory_space=pltpu.VMEM),
        scratch_shapes=scratch,
        compiler_params=pltpu.CompilerParams(
            collective_id=0, has_side_effects=True, vmem_limit_bytes=60 * 2**20
        ),
        name="section",
    )(*args)
    return out.reshape(shape)


def solution(mesh):
    in_specs = (
        P("lev", None, "elem"), P("lev", None, "elem"), P("lev", None, "elem"), P("elem", None),
        P("elem"), P(), P(), P(), P(), P(),
    )
    out_specs = P("lev", None, "elem")
    return jax.shard_map(
        on_device, mesh=mesh, in_specs=in_specs, out_specs=out_specs, check_vma=False
    )
```

```python
import functools
import math

import jax
import jax.numpy as jnp
import numpy as np
from jax import lax
from jax.experimental import pallas as pl
from jax.experimental.pallas import tpu as pltpu
from jax.sharding import PartitionSpec as P

MESH = pl.DeviceIdType.MESH
F32 = jnp.float32
BF16 = jnp.bfloat16
LEV = 4
NL = 18
NODES = 16
ROWS = NL * NODES
NE = 512
BLOCK = 48
TALLER = 24 * NODES
PARTS = ((2, 3), (1,), (0,))
TALL = (144, 80, 80)
EDGE = 48
LEVELS = NL * LEV
UNITS = 512
NT = (((1,), (1,)), ((), ()))


def derivative_table():
    nodes = [-1.0, -1.0 / math.sqrt(5.0), 1.0 / math.sqrt(5.0), 1.0]
    table = np.zeros((4, 4))
    for i in range(4):
        for j in range(4):
            if i == j:
                table[i, j] = sum(1.0 / (nodes[i] - nodes[m]) for m in range(4) if m != i)
            else:
                upper = lower = 1.0
                for m in range(4):
                    if m != i and m != j:
                        upper *= nodes[i] - nodes[m]
                    if m != j:
                        lower *= nodes[j] - nodes[m]
                table[i, j] = upper / lower
    return table


def derivative_blocks():
    table = derivative_table()
    eye4, eye_block = np.eye(4), np.eye(BLOCK // NODES)
    first = np.kron(table, eye4)
    second = np.kron(eye4, table)
    blocks = [0.05 * first, 0.05 * second, 0.005 * (first @ first + second @ second)]
    return np.concatenate([np.kron(eye_block, b) for b in blocks]).astype(np.float32)


def kernel(
    t_hbm, u_hbm, v_hbm, pos_hbm, flag_hbm, d_hbm, w0_hbm, b0_hbm, wi_hbm, bi_hbm, wr_hbm,
    out_v,
    t_v, u_v, v_v, pos_v, flag_v, d_v, w0_v, b0_v, wi_v, bi_v, wr_v,
    q_s, tg_s, ag_s, dd_s, fl_s, w0_s, wi_s, bias_s,
    edge_s, halo_out, halo_in, pre_out, pre_in, add_s, col_s, x_s, h_s, hin_s, sum_s,
    col_out0, col_out1, col_out2, col_in0, col_in1, col_in2,
    heat_out0, heat_out1, heat_out2, heat_in0, heat_in1, heat_in2,
    in_sem, ready, halo_send, halo_recv, col_send, col_recv, heat_send, heat_recv,
    pre_send, pre_recv,
):
    col_out, col_in = (col_out0, col_out1, col_out2), (col_in0, col_in1, col_in2)
    heat_out, heat_in = (heat_out0, heat_out1, heat_out2), (heat_in0, heat_in1, heat_in2)
    me = lax.axis_index("lev")
    elem = lax.axis_index("elem")
    count = lax.axis_size("elem")
    nxt = lax.rem(elem + 1, count)
    prv = lax.rem(elem + count - 1, count)
    peers = [lax.rem(me + d, LEV) for d in (2, 1, 3)]

    loads = {}

    def start(first, pairs):
        for n, (name, src, dst) in enumerate(pairs):
            loads[name] = pltpu.make_async_copy(src, dst, in_sem.at[first + n])
            loads[name].start()

    start(0, [
        ("pos", pos_hbm, pos_v), ("t", t_hbm, t_v), ("u", u_hbm, u_v), ("v", v_hbm, v_v),
        ("d", d_hbm, d_v), ("flag", flag_hbm, flag_v),
    ])

    barrier = pltpu.get_barrier_semaphore()
    for p in peers:
        pl.semaphore_signal(barrier, inc=1, device_id=(elem, p), device_id_type=MESH)
    for q in range(LEV):
        pl.semaphore_signal(barrier, inc=1, device_id=(prv, q), device_id_type=MESH)

    loads.pop("pos").wait()
    slot = lax.rem(pos_v[...] + 64, NE)
    for r in range(0, NE, 128):
        rows = lax.broadcasted_iota(jnp.int32, (128, NE), 0) + r
        q_s[pl.ds(r, 128), :] = jnp.where(rows == slot, 1.0, 0.0).astype(BF16)

    loads.pop("d").wait()
    deriv = d_v[...].astype(BF16)
    loads.pop("t").wait()
    t_hi = t_v[...].astype(BF16)
    loads.pop("u").wait()
    loads.pop("v").wait()
    parts = []
    for b in range(0, ROWS, BLOCK):
        sl = slice(b, b + BLOCK)
        g = jnp.dot(deriv, t_hi[sl], preferred_element_type=F32)
        u = u_v[sl, :].astype(F32)
        v = v_v[sl, :].astype(F32)
        tend = g[2 * BLOCK :] - u * g[:BLOCK] - v * g[BLOCK : 2 * BLOCK]
        parts.append(tend.astype(BF16))
    tend = jnp.concatenate(parts, axis=0)
    tg_s[0, :ROWS] = lax.dot_general(tend, q_s[:128, :], NT, preferred_element_type=F32)

    lane = lax.broadcasted_iota(jnp.int32, (NL, 128), 1)
    left = lane < 64
    inner = lane % 64

    def node(i, j, c):
        return tg_s[c, pl.ds(4 * i + j, NL, stride=NODES), :]

    def along_second(t, i):
        own0, own3 = t[i, 0], t[i, 3]
        after = jnp.where(inner == 63, pltpu.roll(own0, 63, 1), pltpu.roll(own0, 127, 1))
        before = jnp.where(inner == 0, pltpu.roll(own3, 65, 1), pltpu.roll(own3, 1, 1))
        t[i, 3] = (own3 + after) * 0.5
        t[i, 0] = (own0 + before) * 0.5

    edge = {(i, j): node(i, j, 0) for i in (0, 3) for j in range(4)}
    along_second(edge, 0)
    along_second(edge, 3)
    edge_s[...] = jnp.zeros(edge_s.shape, F32)
    for h in range(2):
        even, odd = 2 * h, 2 * h + 1
        edge_s[0, pl.ds(24 * h, NL), :] = jnp.where(left, edge[3, even], pltpu.roll(edge[3, odd], 64, 1))
        edge_s[1, pl.ds(24 * h, NL), :] = jnp.where(left, pltpu.roll(edge[0, even], 64, 1), edge[0, odd])
    halo_out[...] = edge_s[...].astype(BF16)
    pl.semaphore_wait(barrier, 7)
    targets = [lax.rem(me + d, LEV) for d in range(LEV)]
    halo_copies = [
        [
            pltpu.make_async_remote_copy(
                src_ref=halo_out.at[n], dst_ref=halo_in.at[n, me], send_sem=halo_send.at[n, d],
                recv_sem=halo_recv.at[n, d], device_id=(e, q), device_id_type=MESH,
            )
            for d, q in enumerate(targets)
        ]
        for n, e in enumerate((nxt, prv))
    ]
    for copy in halo_copies[0]:
        copy.start()


    def send_back():
        pl.semaphore_wait(ready, LEV)
        for copy in halo_copies[1]:
            copy.start()

    rest = lax.dot_general(tend, q_s[128:, :], NT, preferred_element_type=F32)
    for c in range(1, 4):
        tg_s[c, :ROWS] = rest[:, 128 * (c - 1) : 128 * c]
    loads.pop("flag").wait()
    flags = jnp.broadcast_to(flag_v[...].astype(F32), (16, NE)).astype(BF16)
    t_lo = (t_v[...] - t_hi.astype(F32)).astype(BF16)
    stack = jnp.concatenate([t_hi, t_lo, flags], axis=0)

    def to_slots(first):
        both = lax.dot_general(
            stack, q_s[128 * first : 128 * first + 256, :], NT, preferred_element_type=F32
        )
        for h in range(2):
            lanes = slice(128 * h, 128 * h + 128)
            ag_s[first + h, :ROWS] = both[:ROWS, lanes] + both[ROWS : 2 * ROWS, lanes]
        fl_s[:, pl.ds(128 * first, 256)] = both[2 * ROWS : 2 * ROWS + 8]

    to_slots(2)

    def dss(part, h):
        c = PARTS[part][h]
        t = {(i, j): node(i, j, c) for i in range(4) for j in range(4)}
        for j in range(4):
            own0, own3 = t[0, j], t[3, j]
            near0, near3 = own0, own3
            if c == 0:
                near0 = near3 = jnp.zeros((NL, 128), F32)
            after = pltpu.roll(jnp.where(left, node(0, j, (c + 1) % 4), near0), 64, 1)
            before = pltpu.roll(jnp.where(left, near3, node(3, j, (c + 3) % 4)), 64, 1)
            t[3, j] = (own3 + after) * 0.5
            t[0, j] = (own0 + before) * 0.5
        for i in range(4):
            along_second(t, i)
        col = {}
        for i in range(4):
            for j in range(4):
                p = 4 * i + j
                dd_s[c, p, :NL, :] = t[i, j]
                col[i, j] = ag_s[c, pl.ds(p, NL, stride=NODES), :] + t[i, j]
                col_s[pl.ds(TALL[part] * i + 72 * h + j, NL, stride=4), :] = col[i, j]
        return col

    def exchange(out, into, send, recv):
        copies = []
        for n, p in enumerate(peers):
            copy = pltpu.make_async_remote_copy(
                src_ref=out.at[p], dst_ref=into.at[me], send_sem=send.at[n],
                recv_sem=recv.at[n], device_id=(elem, p), device_id_type=MESH,
            )
            copy.start()
            copies.append(copy)
        into[me] = out[me]
        return copies

    def send_columns(part):
        tall, used = TALL[part], 72 * len(PARTS[part])
        if tall > used:
            for i in range(LEV):
                col_s[pl.ds(tall * i + used, tall - used), :] = jnp.zeros((tall - used, 128), F32)
        col_out[part][...] = col_s[: LEV * tall, :].astype(BF16).reshape(LEV, tall, 128)
        return exchange(col_out[part], col_in[part], col_send.at[part], col_recv.at[part])

    def gate(h):
        return (h + h * jnp.tanh(h)).astype(BF16)

    def layers(x):
        width = x.shape[1]
        row8 = lax.broadcasted_iota(jnp.int32, (8, width), 0)
        x = jnp.concatenate([x, jnp.where(row8 < 2, 1.0, 0.0)], axis=0).astype(BF16)
        hid = gate(jnp.dot(w0_s[:, : LEVELS + 8], x, preferred_element_type=F32))
        for m in range(2):
            pre = jnp.dot(wi_s[pl.ds(m * UNITS, UNITS), :], hid, preferred_element_type=F32)
            hid = gate(pre + jnp.concatenate([bias_s[m]] * (width // 128), axis=1))
        return jnp.dot(wr_v[...], hid, preferred_element_type=F32)

    def network(part, copies):
        size = len(PARTS[part])
        for copy in copies:
            copy.wait_recv()
        for src in range(LEV):
            block = col_in[part][src].astype(F32)
            for h in range(size):
                x_s[pl.ds(288 * h + 72 * src, 72), :] = block[72 * h : 72 * h + 72]
        heat = layers(jnp.concatenate(
            [x_s[pl.ds(288 * h + j, LEVELS, stride=4), :] for j in range(4) for h in range(size)], axis=1
        ))
        for n in range(4 * size):
            j, h = divmod(n, size)
            h_s[pl.ds(288 * h + j, LEVELS, stride=4), :] = heat[:, 128 * n : 128 * n + 128]
        for dst in range(LEV):
            block = [h_s[pl.ds(288 * h + 72 * dst, 72), :] for h in range(size)]
            if size == 1:
                block.append(jnp.zeros((8, 128), F32))
            heat_out[part][dst] = jnp.concatenate(block, axis=0).astype(BF16)
        return exchange(heat_out[part], heat_in[part], heat_send.at[part], heat_recv.at[part])

    def unpack(part, late):
        for q in range(LEV):
            hin_s[: TALL[part], :] = heat_in[part][q].astype(F32)
            for h, c in enumerate(PARTS[part]):
                day = fl_s[pl.ds(0, 1), pl.ds(128 * c, 128)]
                for j in range(4):
                    p = 4 * q + j
                    heat = hin_s[pl.ds(72 * h + j, NL, stride=4), :] * day
                    if c == 0 and q == 0:
                        heat = jnp.where(left, heat, late[j])
                    if c == 0 and q == 3:
                        heat = jnp.where(left, late[j], heat)
                    sum_s[c, pl.ds(p, NL, stride=NODES), :] = dd_s[c, p, :NL, :] + heat

    col_copies = []
    for part, chunks in enumerate(PARTS):
        for h in range(len(chunks)):
            col = dss(part, h)
        col_copies.append(send_columns(part))
        if part == 0:
            start(6, [
                ("w0", w0_hbm, w0_v), ("b0", b0_hbm, b0_v), ("bi", bi_hbm, bi_v),
                ("wi", wi_hbm, wi_v), ("wr", wr_hbm, wr_v),
            ])
            for q in targets:
                pl.semaphore_signal(ready, inc=1, device_id=(nxt, q), device_id_type=MESH)
            to_slots(0)
    col_s[pl.ds(72, 8), :] = jnp.zeros((8, 128), F32)
    for j in range(4):
        col_s[pl.ds(j, NL, stride=4), :] = jnp.where(left, col[3, j], col[0, j])
    pre_out[...] = col_s[:80, :].astype(BF16)
    pre_copies = []
    for n, p in enumerate(peers):
        copy = pltpu.make_async_remote_copy(
            src_ref=pre_out, dst_ref=pre_in.at[me], send_sem=pre_send.at[n],
            recv_sem=pre_recv.at[n], device_id=(elem, p), device_id_type=MESH,
        )
        copy.start()
        pre_copies.append(copy)
    pre_in[me] = pre_out[...]
    closing = lax.rem(elem, count // 2) == 0

    loads.pop("w0").wait()
    loads.pop("b0").wait()
    bias = b0_v[...] * 0.5
    coarse = bias.astype(BF16).astype(F32)
    row8 = lax.broadcasted_iota(jnp.int32, (8, UNITS), 0)
    tail = jnp.where(row8 == 0, coarse, jnp.where(row8 == 1, bias - coarse, 0.0))
    w0 = jnp.concatenate(
        [w0_v[...].astype(F32) * 0.5, tail, jnp.zeros((128 - LEVELS - 8, UNITS), F32)], axis=0
    )
    w0_s[...] = w0.T.astype(BF16)
    loads.pop("bi").wait()
    for m in range(2):
        bias_s[m] = jnp.broadcast_to(bi_v[pl.ds(m, 1), :] * 0.5, (128, UNITS)).T
    loads.pop("wi").wait()
    wi_s[...] = wi_v[...] * jnp.asarray(0.5, BF16)
    loads.pop("wr").wait()

    pl.when(jnp.logical_not(closing))(send_back)
    heat_copies = [network(part, copies) for part, copies in enumerate(col_copies)]

    def accumulate(first, last, base):
        total = jnp.concatenate([sum_s[c, :ROWS] for c in range(first, last)], axis=1).astype(BF16)
        rows = q_s[128 * first : 128 * last, :]
        out_v[...] = base[...] + jnp.dot(total, rows, preferred_element_type=F32)

    def finish(part):
        for copy in heat_copies[part]:
            copy.wait_recv()
        unpack(part, late)

    late = []
    finish(0)
    accumulate(2, 4, t_v)
    pl.when(closing)(send_back)
    for copy in pre_copies:
        copy.wait_recv()
    for src in range(LEV):
        x_s[pl.ds(72 * src, 72), :] = pre_in[src].astype(F32)[:72]
    for copy in halo_copies[0] + halo_copies[1]:
        copy.wait_recv()
    for src in range(LEV):
        below, above = halo_in[0, src].astype(F32), halo_in[1, src].astype(F32)
        for j in range(4):
            row = 24 * (j // 2)
            before, after = below[row : row + NL], above[row : row + NL]
            if j % 2 == 0:
                before = pltpu.roll(before, 64, 1)
            else:
                after = pltpu.roll(after, 64, 1)
            rows = pl.ds(72 * src + j, NL, stride=4)
            add = jnp.where(left, after, before) * 0.5
            add_s[rows, :] = add
            x_s[rows, :] = x_s[rows, :] + add
    heat = layers(
        jnp.concatenate([x_s[pl.ds(j, LEVELS, stride=4), :] for j in range(4)], axis=1)
    )
    for j in range(4):
        h_s[pl.ds(j, LEVELS, stride=4), :] = heat[:, 128 * j : 128 * j + 128]
    day = fl_s[pl.ds(0, 1), pl.ds(0, 128)]
    for j in range(4):
        rows = pl.ds(72 * me + j, NL, stride=4)
        late.append(add_s[rows, :] + h_s[rows, :] * day)
    finish(1)
    finish(2)
    accumulate(0, 2, out_v)

    for copies in halo_copies + col_copies + heat_copies + [pre_copies]:
        for copy in copies:
            copy.wait_send()


def on_device(t, u, v, pos, sunlit, w0, b0, wi, bi, wr):
    shape = t.shape
    args = [
        t.reshape(ROWS, NE), u.reshape(ROWS, NE), v.reshape(ROWS, NE), pos, sunlit.reshape(1, NE),
        jnp.asarray(derivative_blocks()), w0.T, b0.reshape(1, UNITS), wi.reshape(2 * UNITS, UNITS),
        bi, wr,
    ]
    vmem = [pltpu.VMEM(a.shape, a.dtype) for a in args]
    dma = pltpu.SemaphoreType.DMA
    scratch = vmem + [
        pltpu.VMEM((NE, NE), BF16),
        pltpu.VMEM((4, TALLER, 128), F32),
        pltpu.VMEM((4, TALLER, 128), F32),
        pltpu.VMEM((4, NODES, 24, 128), F32),
        pltpu.VMEM((8, NE), F32),
        pltpu.VMEM((UNITS, 128), BF16),
        pltpu.VMEM((2 * UNITS, UNITS), BF16),
        pltpu.VMEM((2, UNITS, 128), F32),
        pltpu.VMEM((2, EDGE, 128), F32),
        pltpu.VMEM((2, EDGE, 128), BF16),
        pltpu.VMEM((2, LEV, EDGE, 128), BF16),
        pltpu.VMEM((80, 128), BF16),
        pltpu.VMEM((LEV, 80, 128), BF16),
        pltpu.VMEM((ROWS + 32, 128), F32),
        pltpu.VMEM((LEV * max(TALL) + 32, 128), F32),
        pltpu.VMEM((2 * ROWS + 32, 128), F32),
        pltpu.VMEM((2 * ROWS + 32, 128), F32),
        pltpu.VMEM((max(TALL) + 32, 128), F32),
        pltpu.VMEM((4, TALLER, 128), F32),
    ]
    scratch += [pltpu.VMEM((LEV, tall, 128), BF16) for _ in range(4) for tall in TALL]
    scratch += [
        dma((len(args),)), pltpu.SemaphoreType.REGULAR, dma((2, LEV)), dma((2, LEV)),
        dma((3, 3)), dma((3, 3)), dma((3, 3)), dma((3, 3)), dma((3,)), dma((3,)),
    ]
    any_spec = pl.BlockSpec(memory_space=pltpu.HBM)
    out = pl.pallas_call(
        kernel,
        out_shape=pltpu.VMEM((ROWS, NE), F32),
        in_specs=[any_spec] * len(args),
        out_specs=pl.BlockSpec(memory_space=pltpu.VMEM),
        scratch_shapes=scratch,
        compiler_params=pltpu.CompilerParams(
            collective_id=0, has_side_effects=True, vmem_limit_bytes=60 * 2**20
        ),
        name="section",
    )(*args)
    return out.reshape(shape)


def solution(mesh):
    in_specs = (
        P("lev", None, "elem"), P("lev", None, "elem"), P("lev", None, "elem"), P("elem", None),
        P("elem"), P(), P(), P(), P(), P(),
    )
    out_specs = P("lev", None, "elem")
    return jax.shard_map(
        on_device, mesh=mesh, in_specs=in_specs, out_specs=out_specs, check_vma=False
    )
```

```python
import functools
import math

import jax
import jax.numpy as jnp
import numpy as np
from jax import lax
from jax.experimental import pallas as pl
from jax.experimental.pallas import tpu as pltpu
from jax.sharding import PartitionSpec as P

MESH = pl.DeviceIdType.MESH
F32 = jnp.float32
BF16 = jnp.bfloat16
LEV = 4
NL = 18
NODES = 16
ROWS = NL * NODES
NE = 512
BLOCK = 48
TALLER = 24 * NODES
PARTS = ((2, 3), (1,), (0,))
TALL = (144, 80, 80)
EDGE = 48
LEVELS = NL * LEV
UNITS = 512
NT = (((1,), (1,)), ((), ()))


def derivative_table():
    nodes = [-1.0, -1.0 / math.sqrt(5.0), 1.0 / math.sqrt(5.0), 1.0]
    table = np.zeros((4, 4))
    for i in range(4):
        for j in range(4):
            if i == j:
                table[i, j] = sum(1.0 / (nodes[i] - nodes[m]) for m in range(4) if m != i)
            else:
                upper = lower = 1.0
                for m in range(4):
                    if m != i and m != j:
                        upper *= nodes[i] - nodes[m]
                    if m != j:
                        lower *= nodes[j] - nodes[m]
                table[i, j] = upper / lower
    return table


def derivative_blocks():
    table = derivative_table()
    eye4, eye_block = np.eye(4), np.eye(BLOCK // NODES)
    first = np.kron(table, eye4)
    second = np.kron(eye4, table)
    blocks = [0.05 * first, 0.05 * second, 0.005 * (first @ first + second @ second)]
    return np.concatenate([np.kron(eye_block, b) for b in blocks]).astype(np.float32)


def kernel(
    t_hbm, u_hbm, v_hbm, pos_hbm, flag_hbm, d_hbm, w0_hbm, b0_hbm, wi_hbm, bi_hbm, wr_hbm,
    out_v,
    t_v, u_v, v_v, pos_v, flag_v, d_v, w0_v, b0_v, wi_v, bi_v, wr_v,
    q_s, tg_s, ag_s, dd_s, fl_s, w0_s, wi_s, bias_s,
    edge_s, halo_out, halo_in, pre_out, pre_in, add_s, col_s, x_s, h_s, hin_s, sum_s,
    col_out0, col_out1, col_out2, col_in0, col_in1, col_in2,
    heat_out0, heat_out1, heat_out2, heat_in0, heat_in1, heat_in2,
    in_sem, ready, halo_send, halo_recv, col_send, col_recv, heat_send, heat_recv,
    pre_send, pre_recv,
):
    col_out, col_in = (col_out0, col_out1, col_out2), (col_in0, col_in1, col_in2)
    heat_out, heat_in = (heat_out0, heat_out1, heat_out2), (heat_in0, heat_in1, heat_in2)
    me = lax.axis_index("lev")
    elem = lax.axis_index("elem")
    count = lax.axis_size("elem")
    nxt = lax.rem(elem + 1, count)
    prv = lax.rem(elem + count - 1, count)
    peers = [lax.rem(me + d, LEV) for d in (2, 1, 3)]

    loads = {}

    def start(first, pairs):
        for n, (name, src, dst) in enumerate(pairs):
            loads[name] = pltpu.make_async_copy(src, dst, in_sem.at[first + n])
            loads[name].start()

    start(0, [
        ("pos", pos_hbm, pos_v), ("t", t_hbm, t_v), ("u", u_hbm, u_v), ("v", v_hbm, v_v),
        ("d", d_hbm, d_v), ("flag", flag_hbm, flag_v),
    ])

    barrier = pltpu.get_barrier_semaphore()
    for p in peers:
        pl.semaphore_signal(barrier, inc=1, device_id=(elem, p), device_id_type=MESH)
    for q in range(LEV):
        pl.semaphore_signal(barrier, inc=1, device_id=(prv, q), device_id_type=MESH)

    loads.pop("pos").wait()
    slot = lax.rem(pos_v[...] + 64, NE)
    for r in range(0, NE, 128):
        rows = lax.broadcasted_iota(jnp.int32, (128, NE), 0) + r
        q_s[pl.ds(r, 128), :] = jnp.where(rows == slot, 1.0, 0.0).astype(BF16)

    loads.pop("d").wait()
    deriv = d_v[...].astype(BF16)
    loads.pop("t").wait()
    t_hi = t_v[...].astype(BF16)
    loads.pop("u").wait()
    loads.pop("v").wait()
    parts = []
    for b in range(0, ROWS, BLOCK):
        sl = slice(b, b + BLOCK)
        g = jnp.dot(deriv, t_hi[sl], preferred_element_type=F32)
        u = u_v[sl, :].astype(F32)
        v = v_v[sl, :].astype(F32)
        tend = g[2 * BLOCK :] - u * g[:BLOCK] - v * g[BLOCK : 2 * BLOCK]
        parts.append(tend.astype(BF16))
    tend = jnp.concatenate(parts, axis=0)
    tg_s[0, :ROWS] = lax.dot_general(tend, q_s[:128, :], NT, preferred_element_type=F32)

    lane = lax.broadcasted_iota(jnp.int32, (NL, 128), 1)
    left = lane < 64
    inner = lane % 64

    def node(i, j, c):
        return tg_s[c, pl.ds(4 * i + j, NL, stride=NODES), :]

    def along_second(t, i):
        own0, own3 = t[i, 0], t[i, 3]
        after = jnp.where(inner == 63, pltpu.roll(own0, 63, 1), pltpu.roll(own0, 127, 1))
        before = jnp.where(inner == 0, pltpu.roll(own3, 65, 1), pltpu.roll(own3, 1, 1))
        t[i, 3] = (own3 + after) * 0.5
        t[i, 0] = (own0 + before) * 0.5

    edge = {(i, j): node(i, j, 0) for i in (0, 3) for j in range(4)}
    along_second(edge, 0)
    along_second(edge, 3)
    edge_s[...] = jnp.zeros(edge_s.shape, F32)
    for h in range(2):
        even, odd = 2 * h, 2 * h + 1
        edge_s[0, pl.ds(24 * h, NL), :] = jnp.where(left, edge[3, even], pltpu.roll(edge[3, odd], 64, 1))
        edge_s[1, pl.ds(24 * h, NL), :] = jnp.where(left, pltpu.roll(edge[0, even], 64, 1), edge[0, odd])
    halo_out[...] = edge_s[...].astype(BF16)
    pl.semaphore_wait(barrier, 7)
    targets = [lax.rem(me + d, LEV) for d in range(LEV)]
    halo_copies = [
        [
            pltpu.make_async_remote_copy(
                src_ref=halo_out.at[n], dst_ref=halo_in.at[n, me], send_sem=halo_send.at[n, d],
                recv_sem=halo_recv.at[n, d], device_id=(e, q), device_id_type=MESH,
            )
            for d, q in enumerate(targets)
        ]
        for n, e in enumerate((nxt, prv))
    ]
    for copy in halo_copies[0]:
        copy.start()


    def send_back():
        pl.semaphore_wait(ready, LEV)
        for copy in halo_copies[1]:
            copy.start()

    rest = lax.dot_general(tend, q_s[128:, :], NT, preferred_element_type=F32)
    for c in range(1, 4):
        tg_s[c, :ROWS] = rest[:, 128 * (c - 1) : 128 * c]
    loads.pop("flag").wait()
    flags = jnp.broadcast_to(flag_v[...].astype(F32), (16, NE)).astype(BF16)
    t_lo = (t_v[...] - t_hi.astype(F32)).astype(BF16)
    stack = jnp.concatenate([t_hi, t_lo, flags], axis=0)

    def to_slots(first):
        both = lax.dot_general(
            stack, q_s[128 * first : 128 * first + 256, :], NT, preferred_element_type=F32
        )
        for h in range(2):
            lanes = slice(128 * h, 128 * h + 128)
            ag_s[first + h, :ROWS] = both[:ROWS, lanes] + both[ROWS : 2 * ROWS, lanes]
        fl_s[:, pl.ds(128 * first, 256)] = both[2 * ROWS : 2 * ROWS + 8]

    to_slots(2)

    def dss(part, h):
        c = PARTS[part][h]
        t = {(i, j): node(i, j, c) for i in range(4) for j in range(4)}
        for j in range(4):
            own0, own3 = t[0, j], t[3, j]
            near0, near3 = own0, own3
            if c == 0:
                near0 = near3 = jnp.zeros((NL, 128), F32)
            after = pltpu.roll(jnp.where(left, node(0, j, (c + 1) % 4), near0), 64, 1)
            before = pltpu.roll(jnp.where(left, near3, node(3, j, (c + 3) % 4)), 64, 1)
            t[3, j] = (own3 + after) * 0.5
            t[0, j] = (own0 + before) * 0.5
        for i in range(4):
            along_second(t, i)
        col = {}
        for i in range(4):
            for j in range(4):
                p = 4 * i + j
                dd_s[c, p, :NL, :] = t[i, j]
                col[i, j] = ag_s[c, pl.ds(p, NL, stride=NODES), :] + t[i, j]
                col_s[pl.ds(TALL[part] * i + 72 * h + j, NL, stride=4), :] = col[i, j]
        return col

    def exchange(out, into, send, recv):
        copies = []
        for n, p in enumerate(peers):
            copy = pltpu.make_async_remote_copy(
                src_ref=out.at[p], dst_ref=into.at[me], send_sem=send.at[n],
                recv_sem=recv.at[n], device_id=(elem, p), device_id_type=MESH,
            )
            copy.start()
            copies.append(copy)
        into[me] = out[me]
        return copies

    def send_columns(part):
        tall, used = TALL[part], 72 * len(PARTS[part])
        if tall > used:
            for i in range(LEV):
                col_s[pl.ds(tall * i + used, tall - used), :] = jnp.zeros((tall - used, 128), F32)
        col_out[part][...] = col_s[: LEV * tall, :].astype(BF16).reshape(LEV, tall, 128)
        return exchange(col_out[part], col_in[part], col_send.at[part], col_recv.at[part])

    def gate(h):
        return (h + h * jnp.tanh(h)).astype(BF16)

    def layers(x):
        width = x.shape[1]
        row8 = lax.broadcasted_iota(jnp.int32, (8, width), 0)
        x = jnp.concatenate([x, jnp.where(row8 < 2, 1.0, 0.0)], axis=0).astype(BF16)
        hid = gate(jnp.dot(w0_s[:, : LEVELS + 8], x, preferred_element_type=F32))
        for m in range(2):
            pre = jnp.dot(wi_s[pl.ds(m * UNITS, UNITS), :], hid, preferred_element_type=F32)
            hid = gate(pre + jnp.concatenate([bias_s[m]] * (width // 128), axis=1))
        return jnp.dot(wr_v[...], hid, preferred_element_type=F32)

    def network(part, copies):
        size = len(PARTS[part])
        for copy in copies:
            copy.wait_recv()
        for src in range(LEV):
            block = col_in[part][src].astype(F32)
            for h in range(size):
                x_s[pl.ds(288 * h + 72 * src, 72), :] = block[72 * h : 72 * h + 72]
        heat = layers(jnp.concatenate(
            [x_s[pl.ds(288 * h + j, LEVELS, stride=4), :] for j in range(4) for h in range(size)], axis=1
        ))
        for n in range(4 * size):
            j, h = divmod(n, size)
            h_s[pl.ds(288 * h + j, LEVELS, stride=4), :] = heat[:, 128 * n : 128 * n + 128]
        for dst in range(LEV):
            block = [h_s[pl.ds(288 * h + 72 * dst, 72), :] for h in range(size)]
            if size == 1:
                block.append(jnp.zeros((8, 128), F32))
            heat_out[part][dst] = jnp.concatenate(block, axis=0).astype(BF16)
        return exchange(heat_out[part], heat_in[part], heat_send.at[part], heat_recv.at[part])

    def unpack(part, late):
        for q in range(LEV):
            hin_s[: TALL[part], :] = heat_in[part][q].astype(F32)
            for h, c in enumerate(PARTS[part]):
                day = fl_s[pl.ds(0, 1), pl.ds(128 * c, 128)]
                for j in range(4):
                    p = 4 * q + j
                    heat = hin_s[pl.ds(72 * h + j, NL, stride=4), :] * day
                    if c == 0 and q == 0:
                        heat = jnp.where(left, heat, late[j])
                    if c == 0 and q == 3:
                        heat = jnp.where(left, late[j], heat)
                    sum_s[c, pl.ds(p, NL, stride=NODES), :] = dd_s[c, p, :NL, :] + heat

    col_copies = []
    for part, chunks in enumerate(PARTS):
        for h in range(len(chunks)):
            col = dss(part, h)
        col_copies.append(send_columns(part))
        if part == 0:
            start(6, [
                ("w0", w0_hbm, w0_v), ("b0", b0_hbm, b0_v), ("bi", bi_hbm, bi_v),
                ("wi", wi_hbm, wi_v), ("wr", wr_hbm, wr_v),
            ])
            for q in targets:
                pl.semaphore_signal(ready, inc=1, device_id=(nxt, q), device_id_type=MESH)
            to_slots(0)
    col_s[pl.ds(72, 8), :] = jnp.zeros((8, 128), F32)
    for j in range(4):
        col_s[pl.ds(j, NL, stride=4), :] = jnp.where(left, col[3, j], col[0, j])
    pre_out[...] = col_s[:80, :].astype(BF16)
    pre_copies = []
    for n, p in enumerate(peers):
        copy = pltpu.make_async_remote_copy(
            src_ref=pre_out, dst_ref=pre_in.at[me], send_sem=pre_send.at[n],
            recv_sem=pre_recv.at[n], device_id=(elem, p), device_id_type=MESH,
        )
        copy.start()
        pre_copies.append(copy)
    pre_in[me] = pre_out[...]
    closing = lax.rem(elem, count // 2) == 0

    loads.pop("w0").wait()
    loads.pop("b0").wait()
    bias = b0_v[...] * 0.5
    coarse = bias.astype(BF16).astype(F32)
    row8 = lax.broadcasted_iota(jnp.int32, (8, UNITS), 0)
    tail = jnp.where(row8 == 0, coarse, jnp.where(row8 == 1, bias - coarse, 0.0))
    w0 = jnp.concatenate(
        [w0_v[...].astype(F32) * 0.5, tail, jnp.zeros((128 - LEVELS - 8, UNITS), F32)], axis=0
    )
    w0_s[...] = w0.T.astype(BF16)
    loads.pop("bi").wait()
    for m in range(2):
        bias_s[m] = jnp.broadcast_to(bi_v[pl.ds(m, 1), :] * 0.5, (128, UNITS)).T
    loads.pop("wi").wait()
    wi_s[...] = wi_v[...] * jnp.asarray(0.5, BF16)
    loads.pop("wr").wait()

    pl.when(jnp.logical_not(closing))(send_back)
    heat_copies = [network(part, copies) for part, copies in enumerate(col_copies)]

    def accumulate(first, last, base):
        total = jnp.concatenate([sum_s[c, :ROWS] for c in range(first, last)], axis=1).astype(BF16)
        rows = q_s[128 * first : 128 * last, :]
        out_v[...] = base[...] + jnp.dot(total, rows, preferred_element_type=F32)

    def finish(part):
        for copy in heat_copies[part]:
            copy.wait_recv()
        unpack(part, late)

    late = []
    finish(0)
    finish(1)
    accumulate(1, 4, t_v)
    pl.when(closing)(send_back)
    for copy in pre_copies:
        copy.wait_recv()
    for src in range(LEV):
        x_s[pl.ds(72 * src, 72), :] = pre_in[src].astype(F32)[:72]
    for copy in halo_copies[0] + halo_copies[1]:
        copy.wait_recv()
    for src in range(LEV):
        below, above = halo_in[0, src].astype(F32), halo_in[1, src].astype(F32)
        for j in range(4):
            row = 24 * (j // 2)
            before, after = below[row : row + NL], above[row : row + NL]
            if j % 2 == 0:
                before = pltpu.roll(before, 64, 1)
            else:
                after = pltpu.roll(after, 64, 1)
            rows = pl.ds(72 * src + j, NL, stride=4)
            add = jnp.where(left, after, before) * 0.5
            add_s[rows, :] = add
            x_s[rows, :] = x_s[rows, :] + add
    heat = layers(
        jnp.concatenate([x_s[pl.ds(j, LEVELS, stride=4), :] for j in range(4)], axis=1)
    )
    for j in range(4):
        h_s[pl.ds(j, LEVELS, stride=4), :] = heat[:, 128 * j : 128 * j + 128]
    day = fl_s[pl.ds(0, 1), pl.ds(0, 128)]
    for j in range(4):
        rows = pl.ds(72 * me + j, NL, stride=4)
        late.append(add_s[rows, :] + h_s[rows, :] * day)
    finish(2)
    accumulate(0, 1, out_v)

    for copies in halo_copies + col_copies + heat_copies + [pre_copies]:
        for copy in copies:
            copy.wait_send()


def on_device(t, u, v, pos, sunlit, w0, b0, wi, bi, wr):
    shape = t.shape
    args = [
        t.reshape(ROWS, NE), u.reshape(ROWS, NE), v.reshape(ROWS, NE), pos, sunlit.reshape(1, NE),
        jnp.asarray(derivative_blocks()), w0.T, b0.reshape(1, UNITS), wi.reshape(2 * UNITS, UNITS),
        bi, wr,
    ]
    vmem = [pltpu.VMEM(a.shape, a.dtype) for a in args]
    dma = pltpu.SemaphoreType.DMA
    scratch = vmem + [
        pltpu.VMEM((NE, NE), BF16),
        pltpu.VMEM((4, TALLER, 128), F32),
        pltpu.VMEM((4, TALLER, 128), F32),
        pltpu.VMEM((4, NODES, 24, 128), F32),
        pltpu.VMEM((8, NE), F32),
        pltpu.VMEM((UNITS, 128), BF16),
        pltpu.VMEM((2 * UNITS, UNITS), BF16),
        pltpu.VMEM((2, UNITS, 128), F32),
        pltpu.VMEM((2, EDGE, 128), F32),
        pltpu.VMEM((2, EDGE, 128), BF16),
        pltpu.VMEM((2, LEV, EDGE, 128), BF16),
        pltpu.VMEM((80, 128), BF16),
        pltpu.VMEM((LEV, 80, 128), BF16),
        pltpu.VMEM((ROWS + 32, 128), F32),
        pltpu.VMEM((LEV * max(TALL) + 32, 128), F32),
        pltpu.VMEM((2 * ROWS + 32, 128), F32),
        pltpu.VMEM((2 * ROWS + 32, 128), F32),
        pltpu.VMEM((max(TALL) + 32, 128), F32),
        pltpu.VMEM((4, TALLER, 128), F32),
    ]
    scratch += [pltpu.VMEM((LEV, tall, 128), BF16) for _ in range(4) for tall in TALL]
    scratch += [
        dma((len(args),)), pltpu.SemaphoreType.REGULAR, dma((2, LEV)), dma((2, LEV)),
        dma((3, 3)), dma((3, 3)), dma((3, 3)), dma((3, 3)), dma((3,)), dma((3,)),
    ]
    any_spec = pl.BlockSpec(memory_space=pltpu.HBM)
    out = pl.pallas_call(
        kernel,
        out_shape=pltpu.VMEM((ROWS, NE), F32),
        in_specs=[any_spec] * len(args),
        out_specs=pl.BlockSpec(memory_space=pltpu.VMEM),
        scratch_shapes=scratch,
        compiler_params=pltpu.CompilerParams(
            collective_id=0, has_side_effects=True, vmem_limit_bytes=60 * 2**20
        ),
        name="section",
    )(*args)
    return out.reshape(shape)


def solution(mesh):
    in_specs = (
        P("lev", None, "elem"), P("lev", None, "elem"), P("lev", None, "elem"), P("elem", None),
        P("elem"), P(), P(), P(), P(), P(),
    )
    out_specs = P("lev", None, "elem")
    return jax.shard_map(
        on_device, mesh=mesh, in_specs=in_specs, out_specs=out_specs, check_vma=False
    )
```
